32 devices in a mesh: groups: 2 (over y), rep: 4 (over x, core), tp: 4 (over z).
Axes of the slice: x: 2, y: 2, z: 4, core: 2. Of those that a mesh axis runs over, the one named last changes fastest.
Arguments:
- tokens: bfloat16 [3072, 8192], P(('groups', 'rep', 'tp')), parts along dimension 0, may hold values from -6 to 6
- base_weight: bfloat16 [8192, 2048], P(None, 'tp'), may hold values from -0.0625 to 0.0625
- delta_codes: bfloat16 [32768, 2048], P(('groups', 'rep'), 'tp'), parts along dimension 0, may hold values from -4 to 4
- delta_scales: bfloat16 [256, 16], P(('groups', 'rep'), 'tp'), parts along dimension 0, may hold values from 0.0019989014 to 0.011962891
- replica_variant: int32 [8], P('groups'), parts along dimension 0, may hold values from 0 to 1
- block_home: int32 [4, 64], P('groups'), parts along dimension 0, may hold values from 0 to 127, as said below
Outputs:
- key_value: bfloat16 [3072, 2048], P(('groups', 'rep'), 'tp'), parts along dimension 0
The draws below stay inside these ranges and needn't reach their ends.
There are 2 independent parts, one for each index of `groups`. The reference program is written for one: setup_inputs(seed, part) draws one part's arguments, and reference() takes and returns one part's arrays. A program takes and returns all parts, laid end to end along the dimension named above; an argument that names none is the same for every part. Nothing has to cross between parts.
Inputs may be any that keep to these rules, and one draw needn't show every extreme that they name: `block_home`: the entries are a permutation of 0 to 127; entry e stands for slot e % 32 of holder e // 32, that is rows e * 128 to (e + 1) * 128 - 1 of delta_codes. At most 24 blocks of one variant lie with one holder, and in every draw some holders hold exactly 24 blocks of a variant.
All inputs are finite; a program needn't handle non-finite values.
Results may differ from the reference program's by a relative error of at most 0.0049.
Values may be sent and summed in bfloat16 or wider, within the bound.
No kernel may reach another device: no remote copies, remote signals or barrier semaphores. Data moves between devices by JAX's collectives and lax.ppermute only.
A program may use at most 128 MiB of HBM per device.

```python
import math
import jax
import jax.numpy as jnp
from jax import lax

D = 8192
BLOCK = 128
HOLDERS = 4
VARIANTS = 2
NB = 64
SLOTS = 32
COLS = 2048
TOK = 384


def draw_block_home(key, part):
    first, second, third = jax.random.split(jax.random.fold_in(key, 7), 3)
    sigma = jax.random.permutation(first, HOLDERS)
    share = NB // HOLDERS
    swing = share // 2
    rows_index = jnp.arange(VARIANTS)
    holder_index = jnp.arange(HOLDERS)
    plus_hot = (holder_index[None, :] == sigma[2 * rows_index][:, None]).astype(jnp.int32)
    minus_hot = (holder_index[None, :] == sigma[2 * rows_index + 1][:, None]).astype(jnp.int32)
    change = plus_hot - minus_hot
    change = change - jnp.roll(change, 1, axis=0)
    counts = share + swing * change

    def spread(count_row):
        return jnp.repeat(holder_index, count_row, total_repeat_length=NB)
    holder_lists = jax.vmap(spread)(counts)
    variant_keys = jax.random.split(second, VARIANTS)
    holder_lists = jax.vmap(jax.random.permutation)(variant_keys, holder_lists)
    flat_holders = holder_lists.reshape(-1).astype(jnp.int32)
    shuffle = jax.random.permutation(third, VARIANTS * NB).astype(jnp.int32)
    score = flat_holders * (VARIANTS * NB) + shuffle
    sorted_index = jnp.argsort(score)
    ranks = jnp.zeros((VARIANTS * NB,), jnp.int32).at[sorted_index].set(jnp.arange(VARIANTS * NB, dtype=jnp.int32))
    return ranks.reshape(VARIANTS, NB)


def plant(array, rng, least, high):
    shape = array.shape
    place = [jax.random.randint(jax.random.fold_in(rng, axis), (), 0, shape[axis]) for axis in range(len(shape))]
    array = array.at[tuple(place)].set(least)
    longest = shape.index(max(shape))
    place[longest] = (place[longest] + 1) % shape[longest]
    return array.at[tuple(place)].set(high)


def block_scale(rng, dims, shards, least, top_value):
    def one(dim, blocks):
        steps = jax.random.uniform(jax.random.fold_in(jax.random.fold_in(rng, 6), dim), (blocks,), jnp.float32, least / len(shards), top_value / len(shards))
        return jnp.repeat(jnp.exp(steps), dims[dim] // blocks).reshape((-1,) + (1,) * (len(dims) - dim - 1))

    gain = one(*shards[0])
    for cut in shards[1:]:
        gain = gain * one(*cut)
    return gain


def scatter_about(own_key, dims, scale, reach, cuts=(), kind=jnp.bfloat16):
    loudness = block_scale(own_key, dims, cuts, -0.22, 0.18) if cuts else 1.0
    array = jax.random.normal(own_key, dims, jnp.float32) * scale * loudness
    return jnp.minimum(jnp.maximum(array, -reach), reach).astype(kind)


def setup_inputs(seed: int = 0, part: int = 0) -> dict:
    splits = jax.random.split(jax.random.key(seed), 7)
    part_splits = jax.random.split(jax.random.fold_in(splits[6], part), 7)
    tokens = scatter_about(part_splits[0], (HOLDERS * TOK, D), 1.0, 6.0, ((0, 16),))
    base_weight = scatter_about(splits[1], (D, COLS), D ** -0.5, 0.0625, ((1, 4),))
    delta_codes = scatter_about(part_splits[2], (HOLDERS * SLOTS * BLOCK, COLS), 1.0, 4.0, ((0, 4), (1, 4)))
    delta_scales = jnp.clip(jnp.exp(math.log(0.011962891) - 1.7892117 * jax.random.uniform(part_splits[3], (HOLDERS * SLOTS, COLS // BLOCK), jnp.float32) ** block_scale(part_splits[3], (HOLDERS * SLOTS, COLS // BLOCK), ((0, 4), (1, 4)), -0.2, 0.2)), 0.0019989014, 0.011962891).astype(jnp.bfloat16)
    replica_variant = plant(jax.random.randint(part_splits[4], (HOLDERS,), 0, VARIANTS), jax.random.fold_in(part_splits[4], 1), 0, VARIANTS - 1).astype(jnp.int32)
    block_home = draw_block_home(jax.random.fold_in(jax.random.fold_in(splits[6], part), 71), part)
    return dict(tokens=tokens, base_weight=base_weight, delta_codes=delta_codes, delta_scales=delta_scales, replica_variant=replica_variant, block_home=block_home)


def reference(tokens, base_weight, delta_codes, delta_scales, replica_variant, block_home):
    code_blocks = delta_codes.reshape(HOLDERS * SLOTS, BLOCK, COLS)
    col_blocks = COLS // BLOCK
    base_float = base_weight.astype(jnp.float32)
    prompts = tokens.reshape(HOLDERS, TOK, D)

    def project_one(inputs_pair):
        prompt, variant = inputs_pair
        homes = block_home[variant]
        code_vals = code_blocks[homes].astype(jnp.float32)
        scales = delta_scales[homes].astype(jnp.float32)
        scale_full = jnp.broadcast_to(scales[:, None, :, None], (NB, BLOCK, col_blocks, BLOCK)).reshape(NB, BLOCK, COLS)
        weight = (base_float + (code_vals * scale_full).reshape(D, COLS)).astype(jnp.bfloat16)
        return jnp.dot(prompt, weight, preferred_element_type=jnp.float32).astype(jnp.bfloat16)

    outputs = lax.map(project_one, (prompts, replica_variant))
    return outputs.reshape(HOLDERS * TOK, COLS)
```

```python
import functools
import jax
import jax.numpy as jnp
from jax import lax
from jax.experimental import pallas as pl
from jax.experimental.pallas import tpu as pltpu
from jax.sharding import PartitionSpec as P

CORES = 2
CHUNK_BLOCKS = 8


def kernel(dims, me_ref, variant_ref, home_ref, scale_ref, base_ref, *refs):
    ranks, reps, block, slots, variants = dims
    token_refs = refs[: 2 * ranks - 1]
    own, rights, lefts = token_refs[0], token_refs[1:ranks], token_refs[ranks:]
    stores = refs[2 * ranks - 1 : 2 * ranks - 1 + reps]
    out_ref, token_buf, base_buf, code_buf, total, sems, code_sems = refs[2 * ranks - 1 + reps :]
    rows = own.shape[0]
    depth = own.shape[1]
    span = CHUNK_BLOCKS * block
    chunks = depth // span
    rank, rep = me_ref[0], me_ref[1]
    variant = variant_ref[rep]

    def base_copy(chunk):
        at = pl.ds(pl.multiple_of(chunk * span, span), span)
        return pltpu.make_async_copy(base_ref.at[at, :], base_buf.at[at, :], sems.at[chunk, ranks])

    def token_copy(chunk, hop, source):
        at = pl.ds(pl.multiple_of(chunk * span, span), span)
        row = pl.multiple_of(lax.rem(rank - hop + ranks, ranks) * rows, rows)
        return pltpu.make_async_copy(
            source.at[:, at], token_buf.at[pl.ds(row, rows), at], sems.at[chunk, hop]
        )

    def code_copy(chunk, index, source, slot):
        return pltpu.make_async_copy(
            source.at[pl.ds(pl.multiple_of(slot * block, block), block), :],
            code_buf.at[pl.ds(pl.multiple_of((chunk * CHUNK_BLOCKS + index) * block, block), block), :],
            code_sems.at[chunk, index],
        )

    @pl.loop(0, chunks)
    def _(chunk):
        base_copy(chunk).start()
        token_copy(chunk, 0, own).start()
        for hop in range(1, ranks):
            from_left = rank >= hop

            @pl.when(from_left)
            def _():
                token_copy(chunk, hop, rights[hop - 1]).start()

            @pl.when(jnp.logical_not(from_left))
            def _():
                token_copy(chunk, hop, lefts[ranks - hop - 1]).start()

        @pl.loop(0, CHUNK_BLOCKS)
        def _(index):
            home = home_ref[variant, chunk * CHUNK_BLOCKS + index]
            holder, slot = home // slots, home % slots
            place = (rep // CORES - holder // CORES + reps // CORES) % (reps // CORES)
            place = place * CORES + (rep % CORES + holder % CORES) % CORES
            for at in range(reps):

                @pl.when(place == at)
                def _():
                    code_copy(chunk, index, stores[at], slot).start()

    total[...] = jnp.zeros_like(total)

    @pl.loop(0, chunks)
    def _(chunk):
        base_copy(chunk).wait()
        for hop in range(ranks):
            token_copy(chunk, hop, own).wait()
        for index in range(CHUNK_BLOCKS):
            code_copy(chunk, index, stores[0], 0).wait()
        merged = []
        for index in range(CHUNK_BLOCKS):
            at = pl.ds(pl.multiple_of(chunk * span + index * block, block), block)
            home = home_ref[variant, chunk * CHUNK_BLOCKS + index]
            delta = code_buf[at, :].astype(jnp.float32) * scale_ref[pl.ds(home, 1), :]
            merged.append((base_buf[at, :].astype(jnp.float32) + delta).astype(jnp.bfloat16))
        at = pl.ds(pl.multiple_of(chunk * span, span), span)
        total[...] += jnp.dot(
            token_buf[:, at], jnp.concatenate(merged, axis=0), preferred_element_type=jnp.float32
        )

    out_ref[...] = total[...].astype(out_ref.dtype)


def local(tokens, base_weight, delta_codes, delta_scales, replica_variant, block_home):
    ranks, reps = lax.axis_size("tp"), lax.axis_size("rep")
    rank, rep = lax.axis_index("tp"), lax.axis_index("rep")
    variants, blocks = block_home.shape
    depth, width = base_weight.shape
    rows = tokens.shape[0]
    block = depth // blocks
    slots = delta_scales.shape[0]
    chips = reps // CORES

    rights, lefts = [tokens], [tokens]
    stores = [delta_codes]
    ring = [(i, (i + CORES) % reps) for i in range(reps)]
    swap = [(i, i // CORES * CORES + (i + 1) % CORES) for i in range(reps)]
    for hop in range(1, ranks):
        rights.append(lax.ppermute(rights[-1], "tp", [(i, i + 1) for i in range(hop - 1, ranks - 1)]))
        lefts.append(lax.ppermute(lefts[-1], "tp", [(i, i - 1) for i in range(1, ranks - hop + 1)]))
    for _ in range(1, chips):
        stores.append(lax.ppermute(stores[-1], "rep", ring))
    placed = []
    for store in stores:
        placed += [store, lax.ppermute(store, "rep", swap)]
    scales = lax.all_gather(delta_scales, "rep", axis=0, tiled=True).astype(jnp.float32)
    scales = jnp.repeat(scales, width // delta_scales.shape[1], axis=1)
    me = jnp.stack([rank, rep]).astype(jnp.int32)

    chunks = blocks // CHUNK_BLOCKS
    smem = pl.BlockSpec(memory_space=pltpu.SMEM)
    whole = pl.BlockSpec(memory_space=pltpu.VMEM)
    hbm = pl.BlockSpec(memory_space=pl.ANY)
    arrays = rights + lefts[1:] + placed
    return pl.pallas_call(
        functools.partial(kernel, (ranks, reps, block, slots, variants)),
        out_shape=jax.ShapeDtypeStruct((ranks * rows, width), jnp.bfloat16),
        in_specs=[smem, smem, smem, whole, hbm] + [hbm] * len(arrays),
        out_specs=whole,
        scratch_shapes=[
            pltpu.VMEM((ranks * rows, depth), jnp.bfloat16),
            pltpu.VMEM((depth, width), jnp.bfloat16),
            pltpu.VMEM((depth, width), jnp.bfloat16),
            pltpu.VMEM((ranks * rows, width), jnp.float32),
            pltpu.SemaphoreType.DMA((chunks, ranks + 1)),
            pltpu.SemaphoreType.DMA((chunks, CHUNK_BLOCKS)),
        ],
        compiler_params=pltpu.CompilerParams(vmem_limit_bytes=56 * 1024 * 1024),
        cost_estimate=pl.CostEstimate(
            flops=2 * ranks * rows * depth * width,
            bytes_accessed=2 * (2 * depth * width + ranks * rows * depth),
            transcendentals=0,
        ),
    )(me, replica_variant, block_home, scales, base_weight, *arrays)


def solution(mesh):
    in_specs = (
        P(("groups", "rep", "tp"), None),
        P(None, "tp"),
        P(("groups", "rep"), "tp"),
        P(("groups", "rep"), "tp"),
        P("groups"),
        P("groups", None),
    )
    out_specs = P(("groups", "rep"), "tp")
    return jax.shard_map(local, mesh=mesh, in_specs=in_specs, out_specs=out_specs, check_vma=False)
```

```python
import functools
import jax
import jax.numpy as jnp
from jax import lax
from jax.experimental import pallas as pl
from jax.experimental.pallas import tpu as pltpu
from jax.sharding import PartitionSpec as P

CORES = 2
CHUNK_BLOCKS = 8


def kernel(dims, me_ref, variant_ref, home_ref, scale_ref, base_ref, *refs):
    ranks, reps, block, slots, cuts = dims
    pieces = len(cuts) - 1
    token_refs = refs[: 2 * ranks - 1]
    own, rights, lefts = token_refs[0], token_refs[1:ranks], token_refs[ranks:]
    stores = refs[2 * ranks - 1 : 2 * ranks - 1 + reps * pieces]
    out_ref, token_buf, base_buf, code_buf, total, sems, code_sems = refs[2 * ranks - 1 + reps * pieces :]
    rows = own.shape[0]
    depth = own.shape[1]
    span = CHUNK_BLOCKS * block
    chunks = depth // span
    rank, rep = me_ref[0], me_ref[1]
    variant = variant_ref[rep]

    def base_copy(chunk):
        at = pl.ds(pl.multiple_of(chunk * span, span), span)
        return pltpu.make_async_copy(base_ref.at[at, :], base_buf.at[at, :], sems.at[chunk, ranks])

    def token_copy(chunk, hop, source):
        at = pl.ds(pl.multiple_of(chunk * span, span), span)
        row = pl.multiple_of(lax.rem(rank - hop + ranks, ranks) * rows, rows)
        return pltpu.make_async_copy(
            source.at[:, at], token_buf.at[pl.ds(row, rows), at], sems.at[chunk, hop]
        )

    def code_copy(chunk, index, source, slot):
        return pltpu.make_async_copy(
            source.at[pl.ds(pl.multiple_of(slot * block, block), block), :],
            code_buf.at[pl.ds(pl.multiple_of((chunk * CHUNK_BLOCKS + index) * block, block), block), :],
            code_sems.at[chunk, index],
        )

    @pl.loop(0, chunks)
    def _(chunk):
        base_copy(chunk).start()
        token_copy(chunk, 0, own).start()
        for hop in range(1, ranks):
            from_left = rank >= hop

            @pl.when(from_left)
            def _():
                token_copy(chunk, hop, rights[hop - 1]).start()

            @pl.when(jnp.logical_not(from_left))
            def _():
                token_copy(chunk, hop, lefts[ranks - hop - 1]).start()

        @pl.loop(0, CHUNK_BLOCKS)
        def _(index):
            home = home_ref[variant, chunk * CHUNK_BLOCKS + index]
            holder, slot = home // slots, home % slots
            place = (rep // CORES - holder // CORES + reps // CORES) % (reps // CORES)
            place = place * CORES + (rep % CORES + holder % CORES) % CORES
            for at in range(reps):
                for piece in range(pieces):
                    low, high = cuts[piece] // block, cuts[piece + 1] // block

                    @pl.when((place == at) & (slot >= low) & (slot < high))
                    def _():
                        code_copy(chunk, index, stores[at * pieces + piece], slot - low).start()

    total[...] = jnp.zeros_like(total)

    @pl.loop(0, chunks)
    def _(chunk):
        base_copy(chunk).wait()
        for hop in range(ranks):
            token_copy(chunk, hop, own).wait()
        for index in range(CHUNK_BLOCKS):
            code_copy(chunk, index, stores[0], 0).wait()
        merged = []
        for index in range(CHUNK_BLOCKS):
            at = pl.ds(pl.multiple_of(chunk * span + index * block, block), block)
            home = home_ref[variant, chunk * CHUNK_BLOCKS + index]
            delta = code_buf[at, :].astype(jnp.float32) * scale_ref[pl.ds(home, 1), :]
            merged.append((base_buf[at, :].astype(jnp.float32) + delta).astype(jnp.bfloat16))
        at = pl.ds(pl.multiple_of(chunk * span, span), span)
        total[...] += jnp.dot(
            token_buf[:, at], jnp.concatenate(merged, axis=0), preferred_element_type=jnp.float32
        )

    out_ref[...] = total[...].astype(out_ref.dtype)


def local(tokens, base_weight, delta_codes, delta_scales, replica_variant, block_home):
    ranks, reps = lax.axis_size("tp"), lax.axis_size("rep")
    rank, rep = lax.axis_index("tp"), lax.axis_index("rep")
    variants, blocks = block_home.shape
    depth, width = base_weight.shape
    rows = tokens.shape[0]
    block = depth // blocks
    slots = delta_scales.shape[0]
    chips = reps // CORES

    ring = [(i, (i + CORES) % reps) for i in range(reps)]
    swap = [(i, i // CORES * CORES + (i + 1) % CORES) for i in range(reps)]
    stages = ranks - 1
    pieces = -(-stages // (chips - 1))
    cuts = [slots * i // pieces * block for i in range(pieces + 1)]
    held = [[delta_codes[cuts[i] : cuts[i + 1]] for i in range(pieces)]]
    held += [[None] * pieces for _ in range(chips - 1)]
    twin = [[None] * pieces for _ in range(chips)]
    rights, lefts = [tokens], [tokens]
    todo = [(hop, piece) for hop in range(1, chips) for piece in range(pieces)]
    ready = [(0, piece) for piece in range(pieces)]
    for stage in range(1, ranks):
        due, todo = todo[: -(-len(todo) // (ranks - stage))], todo[-(-len(todo) // (ranks - stage)) :]
        right = lax.ppermute(rights[-1], "tp", [(i, i + 1) for i in range(stage - 1, ranks - 1)])
        left = lax.ppermute(lefts[-1], "tp", [(i, i - 1) for i in range(1, ranks - stage + 1)])
        sent = [lax.ppermute(held[hop - 1][piece], "rep", ring) for hop, piece in due]
        twins = [lax.ppermute(held[hop][piece], "rep", swap) for hop, piece in ready]
        right, left, sent, twins = lax.optimization_barrier((right, left, sent, twins))
        rights.append(right)
        lefts.append(left)
        for (hop, piece), value in zip(due, sent):
            held[hop][piece] = value
        for (hop, piece), value in zip(ready, twins):
            twin[hop][piece] = value
        ready = due
    for hop, piece in ready:
        twin[hop][piece] = lax.ppermute(held[hop][piece], "rep", swap)
    placed = []
    for hop in range(chips):
        placed += held[hop] + twin[hop]
    scales = lax.all_gather(delta_scales, "rep", axis=0, tiled=True).astype(jnp.float32)
    scales = jnp.repeat(scales, width // delta_scales.shape[1], axis=1)
    me = jnp.stack([rank, rep]).astype(jnp.int32)

    chunks = blocks // CHUNK_BLOCKS
    smem = pl.BlockSpec(memory_space=pltpu.SMEM)
    whole = pl.BlockSpec(memory_space=pltpu.VMEM)
    hbm = pl.BlockSpec(memory_space=pl.ANY)
    arrays = rights + lefts[1:] + placed
    return pl.pallas_call(
        functools.partial(kernel, (ranks, reps, block, slots, tuple(cuts))),
        out_shape=jax.ShapeDtypeStruct((ranks * rows, width), jnp.bfloat16),
        in_specs=[smem, smem, smem, whole, hbm] + [hbm] * len(arrays),
        out_specs=whole,
        scratch_shapes=[
            pltpu.VMEM((ranks * rows, depth), jnp.bfloat16),
            pltpu.VMEM((depth, width), jnp.bfloat16),
            pltpu.VMEM((depth, width), jnp.bfloat16),
            pltpu.VMEM((ranks * rows, width), jnp.float32),
            pltpu.SemaphoreType.DMA((chunks, ranks + 1)),
            pltpu.SemaphoreType.DMA((chunks, CHUNK_BLOCKS)),
        ],
        compiler_params=pltpu.CompilerParams(vmem_limit_bytes=56 * 1024 * 1024),
        cost_estimate=pl.CostEstimate(
            flops=2 * ranks * rows * depth * width,
            bytes_accessed=2 * (2 * depth * width + ranks * rows * depth),
            transcendentals=0,
        ),
    )(me, replica_variant, block_home, scales, base_weight, *arrays)


def solution(mesh):
    in_specs = (
        P(("groups", "rep", "tp"), None),
        P(None, "tp"),
        P(("groups", "rep"), "tp"),
        P(("groups", "rep"), "tp"),
        P("groups"),
        P("groups", None),
    )
    out_specs = P(("groups", "rep"), "tp")
    return jax.shard_map(local, mesh=mesh, in_specs=in_specs, out_specs=out_specs, check_vma=False)
```

```python
import functools
import jax
import jax.numpy as jnp
from jax import lax
from jax.experimental import pallas as pl
from jax.experimental.pallas import tpu as pltpu
from jax.sharding import PartitionSpec as P

CORES = 2
CHUNK_BLOCKS = 8


def gather_kernel(dims, me_ref, variant_ref, home_ref, scale_ref, base_ref, *refs):
    ranks, reps, block, slots, cuts = dims
    pieces = len(cuts) - 1
    token_refs = refs[: 2 * ranks - 1]
    own, rights, lefts = token_refs[0], token_refs[1:ranks], token_refs[ranks:]
    stores = refs[2 * ranks - 1 : 2 * ranks - 1 + reps * pieces]
    out_ref, token_buf, base_buf, code_buf, total, sems, code_sems = refs[2 * ranks - 1 + reps * pieces :]
    rows = own.shape[0]
    depth = own.shape[1]
    span = CHUNK_BLOCKS * block
    chunks = depth // span
    rank, rep = me_ref[0], me_ref[1]
    variant = variant_ref[rep]

    def base_copy(chunk):
        at = pl.ds(pl.multiple_of(chunk * span, span), span)
        return pltpu.make_async_copy(base_ref.at[at, :], base_buf.at[at, :], sems.at[chunk, ranks])

    def token_copy(chunk, hop, source):
        at = pl.ds(pl.multiple_of(chunk * span, span), span)
        row = pl.multiple_of(lax.rem(rank - hop + ranks, ranks) * rows, rows)
        return pltpu.make_async_copy(
            source.at[:, at], token_buf.at[pl.ds(row, rows), at], sems.at[chunk, hop]
        )

    def code_copy(chunk, index, source, slot):
        return pltpu.make_async_copy(
            source.at[pl.ds(pl.multiple_of(slot * block, block), block), :],
            code_buf.at[pl.ds(pl.multiple_of((chunk * CHUNK_BLOCKS + index) * block, block), block), :],
            code_sems.at[chunk, index],
        )

    @pl.loop(0, chunks)
    def _(chunk):
        base_copy(chunk).start()
        token_copy(chunk, 0, own).start()
        for hop in range(1, ranks):
            from_left = rank >= hop

            @pl.when(from_left)
            def _():
                token_copy(chunk, hop, rights[hop - 1]).start()

            @pl.when(jnp.logical_not(from_left))
            def _():
                token_copy(chunk, hop, lefts[ranks - hop - 1]).start()

        @pl.loop(0, CHUNK_BLOCKS)
        def _(index):
            home = home_ref[variant, chunk * CHUNK_BLOCKS + index]
            holder, slot = home // slots, home % slots
            place = (rep // CORES - holder // CORES + reps // CORES) % (reps // CORES)
            place = place * CORES + (rep % CORES + holder % CORES) % CORES
            for at in range(reps):
                for piece in range(pieces):
                    low, high = cuts[piece] // block, cuts[piece + 1] // block

                    @pl.when((place == at) & (slot >= low) & (slot < high))
                    def _():
                        code_copy(chunk, index, stores[at * pieces + piece], slot - low).start()

    total[...] = jnp.zeros_like(total)

    @pl.loop(0, chunks)
    def _(chunk):
        base_copy(chunk).wait()
        for hop in range(ranks):
            token_copy(chunk, hop, own).wait()
        for index in range(CHUNK_BLOCKS):
            code_copy(chunk, index, stores[0], 0).wait()
        merged = []
        for index in range(CHUNK_BLOCKS):
            at = pl.ds(pl.multiple_of(chunk * span + index * block, block), block)
            home = home_ref[variant, chunk * CHUNK_BLOCKS + index]
            delta = code_buf[at, :].astype(jnp.float32) * scale_ref[pl.ds(home, 1), :]
            merged.append((base_buf[at, :].astype(jnp.float32) + delta).astype(jnp.bfloat16))
        at = pl.ds(pl.multiple_of(chunk * span, span), span)
        total[...] += jnp.dot(
            token_buf[:, at], jnp.concatenate(merged, axis=0), preferred_element_type=jnp.float32
        )

    out_ref[...] = total[...].astype(out_ref.dtype)


def gather_deltas(tokens, base_weight, delta_codes, delta_scales, replica_variant, block_home):
    ranks, reps = lax.axis_size("tp"), lax.axis_size("rep")
    rank, rep = lax.axis_index("tp"), lax.axis_index("rep")
    variants, blocks = block_home.shape
    depth, width = base_weight.shape
    rows = tokens.shape[0]
    block = depth // blocks
    slots = delta_scales.shape[0]
    chips = reps // CORES

    ring = [(i, (i + CORES) % reps) for i in range(reps)]
    swap = [(i, i // CORES * CORES + (i + 1) % CORES) for i in range(reps)]
    stages = ranks - 1
    pieces = -(-stages // (chips - 1))
    cuts = [slots * i // pieces * block for i in range(pieces + 1)]
    held = [[delta_codes[cuts[i] : cuts[i + 1]] for i in range(pieces)]]
    held += [[None] * pieces for _ in range(chips - 1)]
    twin = [[None] * pieces for _ in range(chips)]
    rights, lefts = [tokens], [tokens]
    todo = [(hop, piece) for hop in range(1, chips) for piece in range(pieces)]
    ready = [(0, piece) for piece in range(pieces)]
    for stage in range(1, ranks):
        due, todo = todo[: -(-len(todo) // (ranks - stage))], todo[-(-len(todo) // (ranks - stage)) :]
        right = lax.ppermute(rights[-1], "tp", [(i, i + 1) for i in range(stage - 1, ranks - 1)])
        left = lax.ppermute(lefts[-1], "tp", [(i, i - 1) for i in range(1, ranks - stage + 1)])
        sent = [lax.ppermute(held[hop - 1][piece], "rep", ring) for hop, piece in due]
        twins = [lax.ppermute(held[hop][piece], "rep", swap) for hop, piece in ready]
        right, left, sent, twins = lax.optimization_barrier((right, left, sent, twins))
        rights.append(right)
        lefts.append(left)
        for (hop, piece), value in zip(due, sent):
            held[hop][piece] = value
        for (hop, piece), value in zip(ready, twins):
            twin[hop][piece] = value
        ready = due
    for hop, piece in ready:
        twin[hop][piece] = lax.ppermute(held[hop][piece], "rep", swap)
    placed = []
    for hop in range(chips):
        placed += held[hop] + twin[hop]
    scales = lax.all_gather(delta_scales, "rep", axis=0, tiled=True).astype(jnp.float32)
    scales = jnp.repeat(scales, width // delta_scales.shape[1], axis=1)
    me = jnp.stack([rank, rep]).astype(jnp.int32)

    chunks = blocks // CHUNK_BLOCKS
    smem = pl.BlockSpec(memory_space=pltpu.SMEM)
    whole = pl.BlockSpec(memory_space=pltpu.VMEM)
    hbm = pl.BlockSpec(memory_space=pl.ANY)
    arrays = rights + lefts[1:] + placed
    return pl.pallas_call(
        functools.partial(gather_kernel, (ranks, reps, block, slots, tuple(cuts))),
        out_shape=jax.ShapeDtypeStruct((ranks * rows, width), jnp.bfloat16),
        in_specs=[smem, smem, smem, whole, hbm] + [hbm] * len(arrays),
        out_specs=whole,
        scratch_shapes=[
            pltpu.VMEM((ranks * rows, depth), jnp.bfloat16),
            pltpu.VMEM((depth, width), jnp.bfloat16),
            pltpu.VMEM((depth, width), jnp.bfloat16),
            pltpu.VMEM((ranks * rows, width), jnp.float32),
            pltpu.SemaphoreType.DMA((chunks, ranks + 1)),
            pltpu.SemaphoreType.DMA((chunks, CHUNK_BLOCKS)),
        ],
        compiler_params=pltpu.CompilerParams(vmem_limit_bytes=56 * 1024 * 1024),
        cost_estimate=pl.CostEstimate(
            flops=2 * ranks * rows * depth * width,
            bytes_accessed=2 * (2 * depth * width + ranks * rows * depth),
            transcendentals=0,
        ),
    )(me, replica_variant, block_home, scales, base_weight, *arrays)


def survey(home_ref, slots, count_ref):
    holders = count_ref.shape[0]
    for holder in range(holders):
        count_ref[holder] = 0

    @pl.loop(0, home_ref.shape[1])
    def _(index):
        holder = lax.div(home_ref[0, index], slots)
        count_ref[holder] = count_ref[holder] + 1


def plan(variant, front, slots, share, count_ref, table_ref):
    held = [
        jnp.where(variant == 0, count_ref[holder], slots - count_ref[holder])
        for holder in range(2 * CORES)
    ]
    for chip in range(2):
        first, second = held[chip * CORES], held[chip * CORES + 1]
        excess = jnp.maximum(first + second - share, 0)
        move_first = jnp.minimum(jnp.maximum(first - share // CORES, 0), excess)
        move_second = excess - move_first
        keep_first, keep_second = first - move_first, second - move_second
        table_ref[0, chip * CORES] = keep_first
        table_ref[0, chip * CORES + 1] = keep_second
        table_ref[1, chip * CORES] = front
        table_ref[1, chip * CORES + 1] = keep_first
        into = 1 - chip
        kept_there = held[into * CORES] + held[into * CORES + 1]
        table_ref[2, chip * CORES] = kept_there - keep_first
        table_ref[2, chip * CORES + 1] = kept_there + move_first - keep_second


def scan(home_ref, variant, front, slots, table_ref, rank_ref, visit):
    for holder in range(2 * CORES):
        rank_ref[holder] = 0

    @pl.loop(0, home_ref.shape[1])
    def _(index):
        home = home_ref[variant, index]
        holder = lax.div(home, slots)
        slot = home - holder * slots
        order = rank_ref[holder]
        rank_ref[holder] = order + 1
        core = lax.rem(holder, CORES)
        here = lax.div(holder, CORES)
        stays = order < table_ref[0, holder]
        kept = jnp.where(order < front, core * front + order, table_ref[1, holder] + order)
        place = jnp.where(stays, kept, table_ref[2, holder] + order)
        chip = jnp.where(stays, here, 1 - here)
        visit(index, home, holder, slot, order - table_ref[0, holder], chip, place)


VMEM_LIMIT = 56 * 1024 * 1024
SMEM = pl.BlockSpec(memory_space=pltpu.SMEM)
VMEM = pl.BlockSpec(memory_space=pltpu.VMEM)
HBM = pl.BlockSpec(memory_space=pl.ANY)


def table_scratch():
    return [
        pltpu.SMEM((2 * CORES,), jnp.int32),
        pltpu.SMEM((3, 2 * CORES), jnp.int32),
        pltpu.SMEM((2 * CORES,), jnp.int32),
    ]


def split_kernel(dims, variant_ref, home_ref, tokens_ref, mine_ref, other_ref, count, table, rank, sems):
    block, slots, share, front = dims
    rep = lax.axis_index("rep")
    chip = lax.div(rep, CORES)
    variant = variant_ref[rep]
    survey(home_ref, slots, count)
    plan(variant, front, slots, share, count, table)

    def visit(index, home, holder, slot, moved, place_chip, place):
        source = tokens_ref.at[:, pl.ds(pl.multiple_of(index * block, block), block)]
        at = pl.ds(pl.multiple_of(place * block, block), block)

        @pl.when(place_chip == chip)
        def _():
            pltpu.make_async_copy(source, mine_ref.at[:, at], sems.at[0]).start()

        @pl.when(place_chip != chip)
        def _():
            pltpu.make_async_copy(source, other_ref.at[:, at], sems.at[1]).start()

    scan(home_ref, variant, front, slots, table, rank, visit)
    half = tokens_ref.at[:, : share * block]
    pltpu.make_async_copy(half, mine_ref, sems.at[0]).wait()
    pltpu.make_async_copy(half, other_ref, sems.at[1]).wait()


def moved_kernel(dims, home_ref, codes_ref, moved_ref, count, table, rank, sems):
    block, slots, share, front = dims
    rep = lax.axis_index("rep")
    survey(home_ref, slots, count)
    most = moved_ref.shape[0] // block

    def copy(slot, moved):
        return pltpu.make_async_copy(
            codes_ref.at[pl.ds(pl.multiple_of(slot * block, block), block), :],
            moved_ref.at[pl.ds(pl.multiple_of(moved * block, block), block), :],
            sems.at[moved],
        )

    for variant in range(home_ref.shape[0]):
        plan(variant, front, slots, share, count, table)

        def visit(index, home, holder, slot, moved, place_chip, place):
            @pl.when((holder == rep) & (moved >= 0) & (moved < most))
            def _():
                copy(slot, moved).start()

        scan(home_ref, variant, front, slots, table, rank, visit)
        leaving = rank[rep] - table[0, rep]

        @pl.loop(0, jnp.minimum(leaving, most))
        def _(moved):
            copy(0, moved).wait()


def merge_kernel(dims, variant_ref, home_ref, scale_ref, base_ref, own, twin, got, got_twin, out_ref, *scratch):
    block, slots, share, front, chunk_blocks = dims
    base_buf, code_buf, homes, count, table, rank, base_sems, code_sems = scratch
    rep = lax.axis_index("rep")
    chip, core = lax.div(rep, CORES), lax.rem(rep, CORES)
    partner = (1 - chip) * CORES + core
    survey(home_ref, slots, count)
    chunks = 2 * share // chunk_blocks
    span = chunk_blocks * block

    for part, replica in enumerate((partner, rep)):
        variant = variant_ref[replica]
        plan(variant, front, slots, share, count, table)

        def visit(index, home, holder, slot, moved, place_chip, place):
            at = part * share + place
            to = pl.ds(pl.multiple_of(at * block, block), block)

            @pl.when(place_chip == chip)
            def _():
                homes[at] = home
                pltpu.make_async_copy(
                    base_ref.at[pl.ds(pl.multiple_of(index * block, block), block), :],
                    base_buf.at[to, :],
                    base_sems.at[at],
                ).start()
                near = lax.rem(holder, CORES) == core
                local_chip = lax.div(holder, CORES) == chip
                for store, row, chosen in (
                    (own, slot, near & local_chip),
                    (twin, slot, jnp.logical_not(near) & local_chip),
                    (got, moved, near & jnp.logical_not(local_chip)),
                    (got_twin, moved, jnp.logical_not(near | local_chip)),
                ):

                    @pl.when(chosen)
                    def _():
                        pltpu.make_async_copy(
                            store.at[pl.ds(pl.multiple_of(row * block, block), block), :],
                            code_buf.at[to, :],
                            code_sems.at[at],
                        ).start()

        scan(home_ref, variant, front, slots, table, rank, visit)

    @pl.loop(0, 2 * share)
    def _(index):
        at = pl.ds(pl.multiple_of(index * block, block), block)
        pltpu.make_async_copy(base_ref.at[pl.ds(0, block), :], base_buf.at[at, :], base_sems.at[index]).wait()
        pltpu.make_async_copy(own.at[pl.ds(0, block), :], code_buf.at[at, :], code_sems.at[index]).wait()
        delta = code_buf[at, :].astype(jnp.float32) * scale_ref[pl.ds(homes[index], 1), :]
        out_ref[at, :] = (base_buf[at, :].astype(jnp.float32) + delta).astype(jnp.bfloat16)


def product_kernel(dims, weight_ref, *refs):
    ranks, part, span = dims
    token_refs = refs[: 2 * ranks - 1]
    own, rights, lefts = token_refs[0], token_refs[1:ranks], token_refs[ranks:]
    out_ref, token_buf, weight_buf, total, sems = refs[2 * ranks - 1 :]
    rows, depth = own.shape
    chunks = depth // span
    rank = lax.axis_index("tp")

    def weight_copy(chunk):
        return pltpu.make_async_copy(
            weight_ref.at[pl.ds(part * depth + chunk * span, span), :],
            weight_buf.at[pl.ds(chunk * span, span), :],
            sems.at[chunk, ranks],
        )

    def token_copy(chunk, hop, source):
        at = pl.ds(chunk * span, span)
        row = pl.multiple_of(lax.rem(rank - hop + ranks, ranks) * rows, rows)
        return pltpu.make_async_copy(
            source.at[:, at], token_buf.at[pl.ds(row, rows), at], sems.at[chunk, hop]
        )

    for chunk in range(chunks):
        weight_copy(chunk).start()
        token_copy(chunk, 0, own).start()
        for hop in range(1, ranks):
            from_left = rank >= hop

            @pl.when(from_left)
            def _():
                token_copy(chunk, hop, rights[hop - 1]).start()

            @pl.when(jnp.logical_not(from_left))
            def _():
                token_copy(chunk, hop, lefts[ranks - hop - 1]).start()

    for chunk in range(chunks):
        weight_copy(chunk).wait()
        for hop in range(ranks):
            token_copy(chunk, hop, own).wait()
        at = pl.ds(chunk * span, span)
        partial = jnp.dot(token_buf[:, at], weight_buf[at, :], preferred_element_type=jnp.float32)
        if chunk == 0:
            total[...] = partial
        else:
            total[...] += partial
    out_ref[...] = total[...].astype(out_ref.dtype)


def swap_tokens(tokens, base_weight, delta_codes, delta_scales, replica_variant, block_home):
    ranks, reps = lax.axis_size("tp"), lax.axis_size("rep")
    variants, blocks = block_home.shape
    depth, width = base_weight.shape
    rows = tokens.shape[0]
    block = depth // blocks
    slots = delta_scales.shape[0]
    share = blocks // (reps // CORES)
    most = blocks // (2 * reps)
    front = 0
    dims = (block, slots, share, front)
    across = [(i, (i + CORES) % reps) for i in range(reps)]
    swap = [(i, i // CORES * CORES + (i + 1) % CORES) for i in range(reps)]
    params = pltpu.CompilerParams(vmem_limit_bytes=VMEM_LIMIT)

    def tie(*values):
        return lax.optimization_barrier(values)

    def right(value, hop):
        return lax.ppermute(value, "tp", [(i, i + 1) for i in range(hop - 1, ranks - 1)])

    def left(value, hop):
        return lax.ppermute(value, "tp", [(i, i - 1) for i in range(1, ranks - hop + 1)])

    half = jax.ShapeDtypeStruct((rows, share * block), tokens.dtype)
    mine, other = pl.pallas_call(
        functools.partial(split_kernel, dims),
        out_shape=[half, half],
        in_specs=[SMEM, SMEM, HBM],
        out_specs=[HBM, HBM],
        scratch_shapes=table_scratch() + [pltpu.SemaphoreType.DMA((2,))],
        compiler_params=params,
    )(replica_variant, block_home, tokens)
    other = lax.ppermute(other, "rep", across)
    mine_right, mine_left = [mine, right(mine, 1)], [mine, left(mine, 1)]
    twin = lax.ppermute(delta_codes, "rep", swap)
    codes, _ = tie(delta_codes, mine)
    moved = pl.pallas_call(
        functools.partial(moved_kernel, dims),
        out_shape=jax.ShapeDtypeStruct((most * block, width), codes.dtype),
        in_specs=[SMEM, HBM],
        out_specs=HBM,
        scratch_shapes=table_scratch() + [pltpu.SemaphoreType.DMA((most,))],
        compiler_params=params,
    )(block_home, codes)
    got = lax.ppermute(moved, "rep", across)
    other_right, other_left = [other, right(other, 1)], [other, left(other, 1)]
    scales, _ = tie(delta_scales, moved)
    scales = lax.all_gather(scales, "rep", axis=0, tiled=True).astype(jnp.float32)
    scales = jnp.repeat(scales, width // delta_scales.shape[1], axis=1)
    for hop in range(2, ranks):
        last = tie(mine_right[-1], mine_left[-1], other)
        mine_right.append(right(last[0], hop))
        mine_left.append(left(last[1], hop))
        if hop == 2:
            got, _ = tie(got, last[0])
            got_twin = lax.ppermute(got, "rep", swap)
        last = tie(other_right[-1], other_left[-1], last[0], got)
        other_right.append(right(last[0], hop))
        other_left.append(left(last[1], hop))
        if hop == 2:
            codes, twin, got, got_twin, _ = tie(codes, twin, got, got_twin, last[0])
            weights = pl.pallas_call(
                functools.partial(merge_kernel, dims + (CHUNK_BLOCKS,)),
                out_shape=jax.ShapeDtypeStruct((2 * share * block, width), jnp.bfloat16),
                in_specs=[SMEM, SMEM, VMEM] + [HBM] * 5,
                out_specs=VMEM,
                scratch_shapes=[
                    pltpu.VMEM((2 * share * block, width), jnp.bfloat16),
                    pltpu.VMEM((2 * share * block, width), jnp.bfloat16),
                    pltpu.SMEM((2 * share,), jnp.int32),
                ]
                + table_scratch()
                + [pltpu.SemaphoreType.DMA((2 * share,)), pltpu.SemaphoreType.DMA((2 * share,))],
                compiler_params=params,
                cost_estimate=pl.CostEstimate(
                    flops=4 * share * block * width, bytes_accessed=12 * share * block * width, transcendentals=0
                ),
            )(replica_variant, block_home, scales, base_weight, codes, twin, got, got_twin)

    def product(part, rights, lefts, kind):
        span = CHUNK_BLOCKS * block
        arrays = rights + lefts[1:]
        return pl.pallas_call(
            functools.partial(product_kernel, (ranks, part, span)),
            out_shape=jax.ShapeDtypeStruct((ranks * rows, width), kind),
            in_specs=[HBM] * (1 + len(arrays)),
            out_specs=VMEM,
            scratch_shapes=[
                pltpu.VMEM((ranks * rows, share * block), jnp.bfloat16),
                pltpu.VMEM((share * block, width), jnp.bfloat16),
                pltpu.VMEM((ranks * rows, width), jnp.float32),
                pltpu.SemaphoreType.DMA((share // CHUNK_BLOCKS, ranks + 1)),
            ],
            compiler_params=params,
            cost_estimate=pl.CostEstimate(
                flops=2 * ranks * rows * share * block * width,
                bytes_accessed=2 * share * block * (width + ranks * rows),
                transcendentals=0,
            ),
        )(weights, *arrays)

    theirs = product(0, other_right, other_left, jnp.bfloat16)
    back = lax.ppermute(theirs, "rep", across)
    ours = product(1, mine_right, mine_left, jnp.float32)
    return (ours + back.astype(jnp.float32)).astype(jnp.bfloat16)


def local(tokens, base_weight, delta_codes, delta_scales, replica_variant, block_home):
    chips = lax.axis_size("rep") // CORES
    two = chips == 2 and block_home.shape[0] == 2 and lax.axis_size("tp") > 2
    plan_of = swap_tokens if two else gather_deltas
    return plan_of(tokens, base_weight, delta_codes, delta_scales, replica_variant, block_home)


def solution(mesh):
    in_specs = (
        P(("groups", "rep", "tp"), None),
        P(None, "tp"),
        P(("groups", "rep"), "tp"),
        P(("groups", "rep"), "tp"),
        P("groups"),
        P("groups", None),
    )
    out_specs = P(("groups", "rep"), "tp")
    return jax.shard_map(local, mesh=mesh, in_specs=in_specs, out_specs=out_specs, check_vma=False)
```

```python
import functools
import jax
import jax.numpy as jnp
from jax import lax
from jax.experimental import pallas as pl
from jax.experimental.pallas import tpu as pltpu
from jax.sharding import PartitionSpec as P

CORES = 2
CHUNK_BLOCKS = 8


CHAINS = 2
SMEM = pl.BlockSpec(memory_space=pltpu.SMEM)
VMEM = pl.BlockSpec(memory_space=pltpu.VMEM)
HBM = pl.BlockSpec(memory_space=pl.ANY)


def kernel(dims, variant_ref, home_ref, scale_ref, base_ref, *refs):
    ranks, reps, block, slots, cuts = dims
    pieces = len(cuts) - 1
    lanes = 2 * ranks - 1
    token_refs = [refs[chain * lanes : (chain + 1) * lanes] for chain in range(CHAINS)]
    store_refs = refs[CHAINS * lanes : CHAINS * lanes + CORES + (reps - CORES) * pieces]
    out_ref, token_buf, base_buf, code_buf, total, sems, code_sems = refs[-7:]
    rows, depth = token_refs[0][0].shape
    span = CHUNK_BLOCKS * block
    chunks = depth // span
    rank, rep = lax.axis_index("tp"), lax.axis_index("rep")
    chips = reps // CORES
    variant = variant_ref[rep]

    def base_copy(chunk):
        at = pl.ds(pl.multiple_of(chunk * span, span), span)
        return pltpu.make_async_copy(base_ref.at[at, :], base_buf.at[at, :], sems.at[chunk, CHAINS * ranks])

    def token_copy(chunk, chain, hop, source):
        at = pl.ds(pl.multiple_of(chunk * span, span), span)
        origin = lax.rem(rank - hop + ranks, ranks)
        row = pl.multiple_of((origin * CHAINS + chain) * rows, rows)
        return pltpu.make_async_copy(
            source.at[:, at], token_buf.at[pl.ds(row, rows), at], sems.at[chunk, chain * ranks + hop]
        )

    def code_copy(chunk, index, source, slot):
        return pltpu.make_async_copy(
            source.at[pl.ds(pl.multiple_of(slot * block, block), block), :],
            code_buf.at[pl.ds(pl.multiple_of((chunk * CHUNK_BLOCKS + index) * block, block), block), :],
            code_sems.at[chunk, index],
        )

    @pl.loop(0, chunks)
    def _(chunk):
        base_copy(chunk).start()
        for chain in range(CHAINS):
            own, rights, lefts = (
                token_refs[chain][0],
                token_refs[chain][1:ranks],
                token_refs[chain][ranks:],
            )
            token_copy(chunk, chain, 0, own).start()
            for hop in range(1, ranks):
                from_left = rank >= hop

                @pl.when(from_left)
                def _():
                    token_copy(chunk, chain, hop, rights[hop - 1]).start()

                @pl.when(jnp.logical_not(from_left))
                def _():
                    token_copy(chunk, chain, hop, lefts[ranks - hop - 1]).start()

        @pl.loop(0, CHUNK_BLOCKS)
        def _(index):
            home = home_ref[variant, chunk * CHUNK_BLOCKS + index]
            holder = lax.div(home, slots)
            slot = home - holder * slots
            away = lax.rem(lax.div(rep, CORES) - lax.div(holder, CORES) + chips, chips)
            turned = lax.rem(lax.rem(rep, CORES) + lax.rem(holder, CORES), CORES)
            for core in range(CORES):

                @pl.when((away == 0) & (turned == core))
                def _():
                    code_copy(chunk, index, store_refs[core], slot).start()

                for hop in range(1, chips):
                    for piece in range(pieces):
                        low, high = cuts[piece] // block, cuts[piece + 1] // block
                        source = store_refs[CORES + ((hop - 1) * CORES + core) * pieces + piece]

                        @pl.when((away == hop) & (turned == core) & (slot >= low) & (slot < high))
                        def _():
                            code_copy(chunk, index, source, slot - low).start()

    total[...] = jnp.zeros_like(total)

    @pl.loop(0, chunks)
    def _(chunk):
        base_copy(chunk).wait()
        for chain in range(CHAINS):
            for hop in range(ranks):
                token_copy(chunk, chain, hop, token_refs[chain][0]).wait()
        for index in range(CHUNK_BLOCKS):
            code_copy(chunk, index, store_refs[0], 0).wait()
        merged = []
        for index in range(CHUNK_BLOCKS):
            at = pl.ds(pl.multiple_of(chunk * span + index * block, block), block)
            home = home_ref[variant, chunk * CHUNK_BLOCKS + index]
            delta = code_buf[at, :].astype(jnp.float32) * scale_ref[pl.ds(home, 1), :]
            merged.append((base_buf[at, :].astype(jnp.float32) + delta).astype(jnp.bfloat16))
        at = pl.ds(pl.multiple_of(chunk * span, span), span)
        total[...] += jnp.dot(
            token_buf[:, at], jnp.concatenate(merged, axis=0), preferred_element_type=jnp.float32
        )

    out_ref[...] = total[...].astype(out_ref.dtype)


def local(tokens, base_weight, delta_codes, delta_scales, replica_variant, block_home):
    ranks, reps = lax.axis_size("tp"), lax.axis_size("rep")
    blocks = block_home.shape[1]
    depth, width = base_weight.shape
    rows = tokens.shape[0] // CHAINS
    block = depth // blocks
    slots = delta_scales.shape[0]
    chips = reps // CORES
    ring = [(i, (i + CORES) % reps) for i in range(reps)]
    swap = [(i, i // CORES * CORES + (i + 1) % CORES) for i in range(reps)]

    def right(value, hop):
        return lax.ppermute(value, "tp", [(i, i + 1) for i in range(hop - 1, ranks - 1)])

    def left(value, hop):
        return lax.ppermute(value, "tp", [(i, i - 1) for i in range(1, ranks - hop + 1)])

    events = [(hop, chain) for hop in range(1, ranks) for chain in range(CHAINS)]
    pieces = max(len(events) // max(chips - 1, 1), CHAINS)
    cuts = [slots * i // pieces * block for i in range(pieces + 1)]
    moves = [(hop, piece) for hop in range(1, chips) for piece in range(pieces)]
    held = [[delta_codes[cuts[i] : cuts[i + 1]] for i in range(pieces)]]
    held += [[None] * pieces for _ in range(chips - 1)]
    twins = [[None] * pieces for _ in range(chips)]
    halves = [tokens[chain * rows : (chain + 1) * rows] for chain in range(CHAINS)]
    rights, lefts = [[half] for half in halves], [[half] for half in halves]
    flight = []
    for chain in range(CHAINS):
        flight.append((right(halves[chain], 1), left(halves[chain], 1)))
    sent = [lax.ppermute(held[0][piece], "rep", ring) for _, piece in moves[:CHAINS]]
    whole_twin = lax.ppermute(delta_codes, "rep", swap)
    swaps, scales = [], delta_scales
    for index in range(max(len(events), len(moves))):
        landing = flight[:1] if index < len(events) else []
        flight = flight[len(landing) :]
        arrived = (landing, sent[:1], swaps, scales)
        sent = sent[1:]
        landing, came, swapped, scales = lax.optimization_barrier(arrived)
        for came_right, came_left in landing:
            hop, chain = events[index]
            rights[chain].append(came_right)
            lefts[chain].append(came_left)
            if hop + 1 < ranks:
                flight.append((right(came_right, hop + 1), left(came_left, hop + 1)))
        for value in swapped:
            hop, piece = moves[index - 1]
            twins[hop][piece] = value
        swaps = []
        for value in came:
            hop, piece = moves[index]
            held[hop][piece] = value
            swaps.append(lax.ppermute(value, "rep", swap))
        if index + CHAINS < len(moves):
            hop, piece = moves[index + CHAINS]
            sent.append(lax.ppermute(held[hop - 1][piece], "rep", ring))
        if index == 1:
            scales = lax.all_gather(scales, "rep", axis=0, tiled=True).astype(jnp.float32)
            scales = jnp.repeat(scales, width // delta_scales.shape[1], axis=1)
    for value in swaps:
        hop, piece = moves[-1]
        twins[hop][piece] = value

    arrays = []
    for chain in range(CHAINS):
        arrays += rights[chain] + lefts[chain][1:]
    arrays += [delta_codes, whole_twin]
    for hop in range(1, chips):
        arrays += held[hop] + twins[hop]
    chunks = blocks // CHUNK_BLOCKS
    total_rows = ranks * CHAINS * rows
    return pl.pallas_call(
        functools.partial(kernel, (ranks, reps, block, slots, tuple(cuts))),
        out_shape=jax.ShapeDtypeStruct((total_rows, width), jnp.bfloat16),
        in_specs=[SMEM, SMEM, VMEM, HBM] + [HBM] * len(arrays),
        out_specs=VMEM,
        scratch_shapes=[
            pltpu.VMEM((total_rows, depth), jnp.bfloat16),
            pltpu.VMEM((depth, width), jnp.bfloat16),
            pltpu.VMEM((depth, width), jnp.bfloat16),
            pltpu.VMEM((total_rows, width), jnp.float32),
            pltpu.SemaphoreType.DMA((chunks, CHAINS * ranks + 1)),
            pltpu.SemaphoreType.DMA((chunks, CHUNK_BLOCKS)),
        ],
        compiler_params=pltpu.CompilerParams(vmem_limit_bytes=56 * 1024 * 1024),
        cost_estimate=pl.CostEstimate(
            flops=2 * total_rows * depth * width,
            bytes_accessed=2 * (2 * depth * width + total_rows * depth),
            transcendentals=0,
        ),
    )(replica_variant, block_home, scales, base_weight, *arrays)


def solution(mesh):
    in_specs = (
        P(("groups", "rep", "tp"), None),
        P(None, "tp"),
        P(("groups", "rep"), "tp"),
        P(("groups", "rep"), "tp"),
        P("groups"),
        P("groups", None),
    )
    out_specs = P(("groups", "rep"), "tp")
    return jax.shard_map(local, mesh=mesh, in_specs=in_specs, out_specs=out_specs, check_vma=False)
```

```python
import functools
import jax
import jax.numpy as jnp
from jax import lax
from jax.experimental import pallas as pl
from jax.experimental.pallas import tpu as pltpu
from jax.sharding import PartitionSpec as P

CORES = 2
CHUNK_BLOCKS = 8


CHAINS = 2
VMEM_LIMIT = 56 * 1024 * 1024
SMEM = pl.BlockSpec(memory_space=pltpu.SMEM)
VMEM = pl.BlockSpec(memory_space=pltpu.VMEM)
HBM = pl.BlockSpec(memory_space=pl.ANY)
BRIEF = pl.CostEstimate(flops=1, bytes_accessed=1, transcendentals=0)


def merge_kernel(dims, variant_ref, home_ref, scale_ref, base_ref, *refs):
    reps, block, slots, parts = dims
    stores = refs[: len(parts)]
    out_ref, base_buf, code_buf, base_sems, code_sems, out_sems = refs[-6:]
    blocks = home_ref.shape[1]
    chips = reps // CORES
    rep = lax.axis_index("rep")
    variant = variant_ref[rep]

    def rows(index):
        return pl.ds(pl.multiple_of(index * block, block), block)

    def copies(index, store, slot):
        return (
            pltpu.make_async_copy(base_ref.at[rows(index), :], base_buf.at[rows(index), :], base_sems.at[index]),
            pltpu.make_async_copy(store.at[rows(slot), :], code_buf.at[rows(index), :], code_sems.at[index]),
        )

    def result(index):
        return pltpu.make_async_copy(base_buf.at[rows(index), :], out_ref.at[rows(index), :], out_sems.at[index])

    def source(index):
        home = home_ref[variant, index]
        holder = lax.div(home, slots)
        slot = home - holder * slots
        away = lax.rem(lax.div(rep, CORES) - lax.div(holder, CORES) + chips, chips)
        turned = lax.rem(lax.rem(rep, CORES) + lax.rem(holder, CORES), CORES)
        return slot, away, turned

    def chosen(part, slot, away, turned):
        hop, core, low, high = part
        return (away == hop) & (turned == core) & (slot >= low) & (slot < high)

    def any_part(slot, away, turned):
        return functools.reduce(jnp.logical_or, [chosen(part, slot, away, turned) for part in parts])

    @pl.loop(0, blocks)
    def _(index):
        slot, away, turned = source(index)
        for part, store in zip(parts, stores):

            @pl.when(chosen(part, slot, away, turned))
            def _():
                for copy in copies(index, store, slot - part[2]):
                    copy.start()

    @pl.loop(0, blocks)
    def _(index):
        slot, away, turned = source(index)

        @pl.when(any_part(slot, away, turned))
        def _():
            for copy in copies(index, stores[0], 0):
                copy.wait()
            row = (turned * chips + away) * slots + slot
            delta = code_buf[rows(index), :].astype(jnp.float32) * scale_ref[pl.ds(row, 1), :]
            merged = base_buf[rows(index), :].astype(jnp.float32) + delta
            base_buf[rows(index), :] = merged.astype(jnp.bfloat16)
            result(index).start()

    @pl.loop(0, blocks)
    def _(index):
        slot, away, turned = source(index)

        @pl.when(any_part(slot, away, turned))
        def _():
            result(index).wait()


def product_kernel(dims, weight_ref, *refs):
    ranks, span = dims
    lanes = 2 * ranks - 1
    token_refs = [refs[chain * lanes : (chain + 1) * lanes] for chain in range(CHAINS)]
    out_ref, token_buf, weight_buf, total, sems = refs[-5:]
    rows, depth = token_refs[0][0].shape
    chunks = depth // span
    rank = lax.axis_index("tp")

    def weight_copy(chunk):
        at = pl.ds(pl.multiple_of(chunk * span, span), span)
        return pltpu.make_async_copy(weight_ref.at[at, :], weight_buf.at[at, :], sems.at[chunk, CHAINS * ranks])

    def token_copy(chunk, chain, hop, source):
        at = pl.ds(pl.multiple_of(chunk * span, span), span)
        origin = lax.rem(rank - hop + ranks, ranks)
        row = pl.multiple_of((origin * CHAINS + chain) * rows, rows)
        return pltpu.make_async_copy(
            source.at[:, at], token_buf.at[pl.ds(row, rows), at], sems.at[chunk, chain * ranks + hop]
        )

    @pl.loop(0, chunks)
    def _(chunk):
        weight_copy(chunk).start()
        for chain in range(CHAINS):
            own, rights, lefts = (
                token_refs[chain][0],
                token_refs[chain][1:ranks],
                token_refs[chain][ranks:],
            )
            token_copy(chunk, chain, 0, own).start()
            for hop in range(1, ranks):
                from_left = rank >= hop

                @pl.when(from_left)
                def _():
                    token_copy(chunk, chain, hop, rights[hop - 1]).start()

                @pl.when(jnp.logical_not(from_left))
                def _():
                    token_copy(chunk, chain, hop, lefts[ranks - hop - 1]).start()

    total[...] = jnp.zeros_like(total)

    @pl.loop(0, chunks)
    def _(chunk):
        weight_copy(chunk).wait()
        for chain in range(CHAINS):
            for hop in range(ranks):
                token_copy(chunk, chain, hop, token_refs[chain][0]).wait()
        at = pl.ds(pl.multiple_of(chunk * span, span), span)
        total[...] += jnp.dot(token_buf[:, at], weight_buf[at, :], preferred_element_type=jnp.float32)

    out_ref[...] = total[...].astype(out_ref.dtype)


def local(tokens, base_weight, delta_codes, delta_scales, replica_variant, block_home):
    ranks, reps = lax.axis_size("tp"), lax.axis_size("rep")
    blocks = block_home.shape[1]
    depth, width = base_weight.shape
    rows = tokens.shape[0] // CHAINS
    block = depth // blocks
    slots, col_blocks = delta_scales.shape
    chips = reps // CORES
    ring = [(i, (i + CORES) % reps) for i in range(reps)]
    swap = [(i, i // CORES * CORES + (i + 1) % CORES) for i in range(reps)]

    def tie(values):
        return lax.optimization_barrier(values)

    def right(value, hop):
        return lax.ppermute(value, "tp", [(i, i + 1) for i in range(hop - 1, ranks - 1)])

    def left(value, hop):
        return lax.ppermute(value, "tp", [(i, i - 1) for i in range(1, ranks - hop + 1)])

    def step(chain, hop):
        return right(rights[chain][-1], hop), left(lefts[chain][-1], hop)

    halves = [tokens[chain * rows : (chain + 1) * rows] for chain in range(CHAINS)]
    rights, lefts = [[half] for half in halves], [[half] for half in halves]
    events = [(hop, chain) for hop in range(1, ranks) for chain in range(CHAINS)]
    most = slots * 3 // 4
    tail_cuts = [most, (most + slots) // 2, slots]
    tails = list(zip(tail_cuts[:-1], tail_cuts[1:]))
    near_last = len(events) - 3
    turns = [near_last * hop // (chips - 1) for hop in range(1, chips)]

    def cut(store, low, high):
        return store[low * block : high * block]

    def across(store):
        return lax.ppermute(store, "rep", ring)

    def turn(store):
        return lax.ppermute(store, "rep", swap)

    flight = [step(chain, 1) for chain in range(CHAINS)]
    bounds = [slots] * (chips - 2) + [most]
    heads, head_twins, source = [], [], delta_codes
    sent = [across(cut(source, 0, bounds[0]))]
    own_twin = turn(delta_codes)
    scale_parts = [delta_scales]
    for _ in range(1, chips):
        scale_parts.append(across(scale_parts[-1]))
    near = jnp.concatenate(scale_parts, axis=0)
    near_twin = turn(near)

    for index, (hop, chain) in enumerate(events[: near_last + 1]):
        came = sent if index in turns else []
        rights[chain].append(flight[0][0])
        lefts[chain].append(flight[0][1])
        flight = flight[1:]
        if index == 1:
            near, near_twin, rights, lefts = tie((near, near_twin, rights, lefts))
        came, rights, lefts = tie((came, rights, lefts))
        if hop + 1 < ranks:
            flight.append(step(chain, hop + 1))
        if index == near_last:
            source, rights, lefts = tie((source, rights, lefts))
        if came:
            heads.append(came[0])
            if len(heads) < chips - 1:
                source = came[0]
                sent = [across(cut(source, 0, bounds[len(heads)]))]
            else:
                sent = [across(cut(source, *ends)) for ends in tails]
            head_twins.append(turn(came[0]))

    near, near_twin = near.astype(jnp.float32), near_twin.astype(jnp.float32)
    both = jnp.concatenate([near, near_twin], axis=0)
    scales = jnp.repeat(both, width // col_blocks, axis=1)

    def merge(weight, parts, stores):
        inputs = [replica_variant, block_home, scales, base_weight] + stores
        given = [] if weight is None else [weight]
        return pl.pallas_call(
            functools.partial(merge_kernel, (reps, block, slots, tuple(parts))),
            out_shape=jax.ShapeDtypeStruct((depth, width), jnp.bfloat16),
            in_specs=[SMEM, SMEM, VMEM] + [HBM] * (1 + len(stores) + len(given)),
            out_specs=HBM,
            scratch_shapes=[
                pltpu.VMEM((depth, width), jnp.bfloat16),
                pltpu.VMEM((depth, width), jnp.bfloat16),
                pltpu.SemaphoreType.DMA((blocks,)),
                pltpu.SemaphoreType.DMA((blocks,)),
                pltpu.SemaphoreType.DMA((blocks,)),
            ],
            input_output_aliases={len(inputs): 0} if given else {},
            compiler_params=pltpu.CompilerParams(vmem_limit_bytes=VMEM_LIMIT),
            cost_estimate=BRIEF,
        )(*inputs, *given)

    parts = [(0, core, 0, slots) for core in range(CORES)]
    own_twin, rights, lefts = tie((own_twin, rights, lefts))
    weight = merge(None, parts, [delta_codes, own_twin])
    sent, weight = tie((sent, weight))
    came = sent
    came_twins = [turn(value) for value in came]
    parts = [(hop, core, 0, high) for core in range(CORES) for hop, high in enumerate(bounds, 1)]
    weight = merge(weight, parts, heads + head_twins)
    parts = [(chips - 1, core, low, high) for core in range(CORES) for low, high in tails]
    weight = merge(weight, parts, came + came_twins)
    flight, weight = tie((flight, weight))
    for (hop, chain), landing in zip(events[near_last + 1 :], flight):
        rights[chain].append(landing[0])
        lefts[chain].append(landing[1])

    arrays = []
    for chain in range(CHAINS):
        arrays += rights[chain] + lefts[chain][1:]
    total_rows = ranks * CHAINS * rows
    chunks = blocks // CHUNK_BLOCKS
    return pl.pallas_call(
        functools.partial(product_kernel, (ranks, CHUNK_BLOCKS * block)),
        out_shape=jax.ShapeDtypeStruct((total_rows, width), jnp.bfloat16),
        in_specs=[HBM] * (1 + len(arrays)),
        out_specs=VMEM,
        scratch_shapes=[
            pltpu.VMEM((total_rows, depth), jnp.bfloat16),
            pltpu.VMEM((depth, width), jnp.bfloat16),
            pltpu.VMEM((total_rows, width), jnp.float32),
            pltpu.SemaphoreType.DMA((chunks, CHAINS * ranks + 1)),
        ],
        compiler_params=pltpu.CompilerParams(vmem_limit_bytes=VMEM_LIMIT),
        cost_estimate=BRIEF,
    )(weight, *arrays)


def solution(mesh):
    in_specs = (
        P(("groups", "rep", "tp"), None),
        P(None, "tp"),
        P(("groups", "rep"), "tp"),
        P(("groups", "rep"), "tp"),
        P("groups"),
        P("groups", None),
    )
    out_specs = P(("groups", "rep"), "tp")
    return jax.shard_map(local, mesh=mesh, in_specs=in_specs, out_specs=out_specs, check_vma=False)
```

```python
import functools
import jax
import jax.numpy as jnp
from jax import lax
from jax.experimental import pallas as pl
from jax.experimental.pallas import tpu as pltpu
from jax.sharding import PartitionSpec as P

CORES = 2
CHUNK_BLOCKS = 8


CHAINS = 2
VMEM_LIMIT = 56 * 1024 * 1024
SMEM = pl.BlockSpec(memory_space=pltpu.SMEM)
VMEM = pl.BlockSpec(memory_space=pltpu.VMEM)
HBM = pl.BlockSpec(memory_space=pl.ANY)
BRIEF = pl.CostEstimate(flops=1, bytes_accessed=1, transcendentals=0)


def scale_kernel(block, scale_ref, codes_ref, *out_refs):
    col_blocks = scale_ref.shape[1]
    wide = codes_ref.shape[1] // col_blocks
    first = 0
    for out_ref in out_refs:
        count = out_ref.shape[0] // block

        @pl.loop(0, count)
        def _(index):
            source = pl.ds(pl.multiple_of((first + index) * block, block), block)
            target = pl.ds(pl.multiple_of(index * block, block), block)
            for col in range(col_blocks):
                at = pl.ds(col * wide, wide)
                delta = codes_ref[source, at].astype(jnp.float32) * scale_ref[first + index, col]
                out_ref[target, at] = delta.astype(jnp.bfloat16)

        first += count


def merge_kernel(block, parts, row_ref, base_ref, *refs):
    stores = refs[: len(parts)]
    out_ref, base_buf, delta_buf, base_sems, delta_sems, out_sems = refs[-6:]
    blocks = row_ref.shape[0]

    def rows(index):
        return pl.ds(pl.multiple_of(index * block, block), block)

    def copies(index, store, slot):
        return (
            pltpu.make_async_copy(base_ref.at[rows(index), :], base_buf.at[rows(index), :], base_sems.at[index]),
            pltpu.make_async_copy(store.at[rows(slot), :], delta_buf.at[rows(index), :], delta_sems.at[index]),
        )

    def result(index):
        return pltpu.make_async_copy(base_buf.at[rows(index), :], out_ref.at[rows(index), :], out_sems.at[index])

    def inside(row, part):
        return (row >= part[0]) & (row < part[1])

    def present(index):
        row = row_ref[index]
        return functools.reduce(jnp.logical_or, [inside(row, part) for part in parts])

    @pl.loop(0, blocks)
    def _(index):
        row = row_ref[index]
        for part, store in zip(parts, stores):

            @pl.when(inside(row, part))
            def _():
                for copy in copies(index, store, row - part[0]):
                    copy.start()

    @pl.loop(0, blocks)
    def _(index):
        @pl.when(present(index))
        def _():
            for copy in copies(index, stores[0], 0):
                copy.wait()
            merged = base_buf[rows(index), :].astype(jnp.float32) + delta_buf[rows(index), :].astype(jnp.float32)
            base_buf[rows(index), :] = merged.astype(jnp.bfloat16)
            result(index).start()

    @pl.loop(0, blocks)
    def _(index):
        @pl.when(present(index))
        def _():
            result(index).wait()


def product_kernel(ranks, span, weight_ref, *refs):
    gathered = refs[:CHAINS]
    out_ref, token_buf, weight_buf, total, sems = refs[CHAINS:]
    height, depth = gathered[0].shape
    rows = height // ranks
    chunks = depth // span

    def copies(chunk):
        at = pl.ds(pl.multiple_of(chunk * span, span), span)
        yield pltpu.make_async_copy(weight_ref.at[at, :], weight_buf.at[at, :], sems.at[chunk, CHAINS])
        for chain, source in enumerate(gathered):
            target = token_buf.at[pl.ds(chain * height, height), at]
            yield pltpu.make_async_copy(source.at[:, at], target, sems.at[chunk, chain])

    @pl.loop(0, chunks)
    def _(chunk):
        for copy in copies(chunk):
            copy.start()

    total[...] = jnp.zeros_like(total)

    @pl.loop(0, chunks)
    def _(chunk):
        for copy in copies(chunk):
            copy.wait()
        at = pl.ds(pl.multiple_of(chunk * span, span), span)
        total[...] += jnp.dot(token_buf[:, at], weight_buf[at, :], preferred_element_type=jnp.float32)

    for chain in range(CHAINS):
        for origin in range(ranks):
            source = pl.ds(chain * height + origin * rows, rows)
            out_ref[pl.ds((origin * CHAINS + chain) * rows, rows), :] = total[source, :].astype(out_ref.dtype)


def local(tokens, base_weight, delta_codes, delta_scales, replica_variant, block_home):
    ranks, reps = lax.axis_size("tp"), lax.axis_size("rep")
    blocks = block_home.shape[1]
    depth, width = base_weight.shape
    rows = tokens.shape[0] // CHAINS
    block = depth // blocks
    slots = delta_scales.shape[0]
    rep = lax.axis_index("rep")
    chips = reps // CORES
    ring = [(i, (i + CORES) % reps) for i in range(reps)]
    swap = [(i, i // CORES * CORES + (i + 1) % CORES) for i in range(reps)]

    halves = [tokens[chain * rows : (chain + 1) * rows] for chain in range(CHAINS)]
    gathered = [lax.all_gather(half, "tp", axis=0, tiled=True) for half in halves]
    cuts = [0, slots * 3 // 4, slots]
    pieces = len(cuts) - 1

    def across(store):
        return lax.ppermute(store, "rep", ring)

    def turn(store):
        return lax.ppermute(store, "rep", swap)

    homes = block_home[replica_variant[rep]]
    holder = homes // slots
    away = (rep // CORES - holder // CORES + chips) % chips
    turned = (rep % CORES + holder % CORES) % CORES
    row_of = (turned * chips + away) * slots + homes % slots

    deltas = pl.pallas_call(
        functools.partial(scale_kernel, block),
        out_shape=[
            jax.ShapeDtypeStruct(((high - low) * block, width), jnp.bfloat16)
            for low, high in zip(cuts[:-1], cuts[1:])
        ],
        in_specs=[SMEM, VMEM],
        out_specs=[VMEM] * pieces,
        compiler_params=pltpu.CompilerParams(vmem_limit_bytes=VMEM_LIMIT),
        cost_estimate=BRIEF,
    )(delta_scales.astype(jnp.float32), delta_codes)
    held, twins = [deltas], [[turn(delta) for delta in deltas]]
    for _ in range(1, chips):
        held.append([across(value) for value in held[-1]])
        twins.append([turn(value) for value in held[-1]])

    def merge(weight, chosen):
        parts, stores = [], []
        for core, kept in enumerate((held, twins)):
            for hop, piece in chosen:
                place = (core * chips + hop) * slots
                parts.append((place + cuts[piece], place + cuts[piece + 1]))
                stores.append(kept[hop][piece])
        inputs = [row_of, base_weight] + stores
        given = [] if weight is None else [weight]
        return pl.pallas_call(
            functools.partial(merge_kernel, block, tuple(parts)),
            out_shape=jax.ShapeDtypeStruct((depth, width), jnp.bfloat16),
            in_specs=[SMEM] + [HBM] * (1 + len(stores) + len(given)),
            out_specs=HBM,
            scratch_shapes=[
                pltpu.VMEM((depth, width), jnp.bfloat16),
                pltpu.VMEM((depth, width), jnp.bfloat16),
                pltpu.SemaphoreType.DMA((blocks,)),
                pltpu.SemaphoreType.DMA((blocks,)),
                pltpu.SemaphoreType.DMA((blocks,)),
            ],
            input_output_aliases={len(inputs): 0} if given else {},
            compiler_params=pltpu.CompilerParams(vmem_limit_bytes=VMEM_LIMIT),
            cost_estimate=BRIEF,
        )(*inputs, *given)

    last = [(chips - 1, piece) for piece in range(1, pieces)]
    early = [(hop, piece) for hop in range(chips) for piece in range(pieces) if (hop, piece) not in last]
    weight = merge(merge(None, early), last)
    gathered, weight = lax.optimization_barrier((gathered, weight))
    total_rows = ranks * CHAINS * rows
    chunks = blocks // CHUNK_BLOCKS
    return pl.pallas_call(
        functools.partial(product_kernel, ranks, CHUNK_BLOCKS * block),
        out_shape=jax.ShapeDtypeStruct((total_rows, width), jnp.bfloat16),
        in_specs=[HBM] * (1 + CHAINS),
        out_specs=VMEM,
        scratch_shapes=[
            pltpu.VMEM((total_rows, depth), jnp.bfloat16),
            pltpu.VMEM((depth, width), jnp.bfloat16),
            pltpu.VMEM((total_rows, width), jnp.float32),
            pltpu.SemaphoreType.DMA((chunks, CHAINS + 1)),
        ],
        compiler_params=pltpu.CompilerParams(vmem_limit_bytes=VMEM_LIMIT),
        cost_estimate=BRIEF,
    )(weight, *gathered)


def solution(mesh):
    in_specs = (
        P(("groups", "rep", "tp"), None),
        P(None, "tp"),
        P(("groups", "rep"), "tp"),
        P(("groups", "rep"), "tp"),
        P("groups"),
        P("groups", None),
    )
    out_specs = P(("groups", "rep"), "tp")
    return jax.shard_map(local, mesh=mesh, in_specs=in_specs, out_specs=out_specs, check_vma=False)
```

```python
import functools
import jax
import jax.numpy as jnp
from jax import lax
from jax.experimental import pallas as pl
from jax.experimental.pallas import tpu as pltpu
from jax.sharding import PartitionSpec as P

CORES = 2
CHUNK_BLOCKS = 8


CHAINS = 1
VMEM_LIMIT = 56 * 1024 * 1024
SMEM = pl.BlockSpec(memory_space=pltpu.SMEM)
VMEM = pl.BlockSpec(memory_space=pltpu.VMEM)
HBM = pl.BlockSpec(memory_space=pl.ANY)
BRIEF = pl.CostEstimate(flops=1, bytes_accessed=1, transcendentals=0)


def scale_kernel(block, scale_ref, codes_ref, *out_refs):
    col_blocks = scale_ref.shape[1]
    wide = codes_ref.shape[1] // col_blocks
    first = 0
    for out_ref in out_refs:
        count = out_ref.shape[0] // block

        @pl.loop(0, count)
        def _(index):
            source = pl.ds(pl.multiple_of((first + index) * block, block), block)
            target = pl.ds(pl.multiple_of(index * block, block), block)
            for col in range(col_blocks):
                at = pl.ds(col * wide, wide)
                delta = codes_ref[source, at].astype(jnp.float32) * scale_ref[first + index, col]
                out_ref[target, at] = delta.astype(jnp.bfloat16)

        first += count


def merge_kernel(block, parts, row_ref, base_ref, *refs):
    stores = refs[: len(parts)]
    out_ref, base_buf, delta_buf, base_sems, delta_sems, out_sems = refs[-6:]
    blocks = row_ref.shape[0]

    def rows(index):
        return pl.ds(pl.multiple_of(index * block, block), block)

    def copies(index, store, slot):
        return (
            pltpu.make_async_copy(base_ref.at[rows(index), :], base_buf.at[rows(index), :], base_sems.at[index]),
            pltpu.make_async_copy(store.at[rows(slot), :], delta_buf.at[rows(index), :], delta_sems.at[index]),
        )

    def result(index):
        return pltpu.make_async_copy(base_buf.at[rows(index), :], out_ref.at[rows(index), :], out_sems.at[index])

    def inside(row, part):
        return (row >= part[0]) & (row < part[1])

    def present(index):
        row = row_ref[index]
        return functools.reduce(jnp.logical_or, [inside(row, part) for part in parts])

    @pl.loop(0, blocks)
    def _(index):
        row = row_ref[index]
        for part, store in zip(parts, stores):

            @pl.when(inside(row, part))
            def _():
                for copy in copies(index, store, row - part[0]):
                    copy.start()

    @pl.loop(0, blocks)
    def _(index):
        @pl.when(present(index))
        def _():
            for copy in copies(index, stores[0], 0):
                copy.wait()
            merged = base_buf[rows(index), :].astype(jnp.float32) + delta_buf[rows(index), :].astype(jnp.float32)
            base_buf[rows(index), :] = merged.astype(jnp.bfloat16)
            result(index).start()

    @pl.loop(0, blocks)
    def _(index):
        @pl.when(present(index))
        def _():
            result(index).wait()


def product_kernel(dims, weight_ref, *refs):
    ranks, span = dims
    lanes = 2 * ranks - 1
    token_refs = [refs[chain * lanes : (chain + 1) * lanes] for chain in range(CHAINS)]
    out_ref, token_buf, weight_buf, total, sems = refs[-5:]
    rows, depth = token_refs[0][0].shape
    chunks = depth // span
    rank = lax.axis_index("tp")

    def weight_copy(chunk):
        at = pl.ds(pl.multiple_of(chunk * span, span), span)
        return pltpu.make_async_copy(weight_ref.at[at, :], weight_buf.at[at, :], sems.at[chunk, CHAINS * ranks])

    def token_copy(chunk, chain, hop, source):
        at = pl.ds(pl.multiple_of(chunk * span, span), span)
        origin = lax.rem(rank - hop + ranks, ranks)
        row = pl.multiple_of((origin * CHAINS + chain) * rows, rows)
        return pltpu.make_async_copy(
            source.at[:, at], token_buf.at[pl.ds(row, rows), at], sems.at[chunk, chain * ranks + hop]
        )

    @pl.loop(0, chunks)
    def _(chunk):
        weight_copy(chunk).start()
        for chain in range(CHAINS):
            own, rights, lefts = (
                token_refs[chain][0],
                token_refs[chain][1:ranks],
                token_refs[chain][ranks:],
            )
            token_copy(chunk, chain, 0, own).start()
            for hop in range(1, ranks):
                from_left = rank >= hop

                @pl.when(from_left)
                def _():
                    token_copy(chunk, chain, hop, rights[hop - 1]).start()

                @pl.when(jnp.logical_not(from_left))
                def _():
                    token_copy(chunk, chain, hop, lefts[ranks - hop - 1]).start()

    total[...] = jnp.zeros_like(total)

    @pl.loop(0, chunks)
    def _(chunk):
        weight_copy(chunk).wait()
        for chain in range(CHAINS):
            for hop in range(ranks):
                token_copy(chunk, chain, hop, token_refs[chain][0]).wait()
        at = pl.ds(pl.multiple_of(chunk * span, span), span)
        total[...] += jnp.dot(token_buf[:, at], weight_buf[at, :], preferred_element_type=jnp.float32)

    out_ref[...] = total[...].astype(out_ref.dtype)


def local(tokens, base_weight, delta_codes, delta_scales, replica_variant, block_home):
    ranks, reps = lax.axis_size("tp"), lax.axis_size("rep")
    blocks = block_home.shape[1]
    depth, width = base_weight.shape
    rows = tokens.shape[0] // CHAINS
    block = depth // blocks
    slots = delta_scales.shape[0]
    rep = lax.axis_index("rep")
    chips = reps // CORES
    ring = [(i, (i + CORES) % reps) for i in range(reps)]
    swap = [(i, i // CORES * CORES + (i + 1) % CORES) for i in range(reps)]

    def tie(values):
        return lax.optimization_barrier(values)

    def right(value, hop):
        return lax.ppermute(value, "tp", [(i, i + 1) for i in range(hop - 1, ranks - 1)])

    def left(value, hop):
        return lax.ppermute(value, "tp", [(i, i - 1) for i in range(1, ranks - hop + 1)])

    def step(chain, hop):
        return right(rights[chain][-1], hop), left(lefts[chain][-1], hop)

    halves = [tokens[chain * rows : (chain + 1) * rows] for chain in range(CHAINS)]
    rights, lefts = [[half] for half in halves], [[half] for half in halves]
    events = [(hop, chain) for hop in range(1, ranks) for chain in range(CHAINS)]
    most = slots * 3 // 4
    cuts = [0, most, slots]
    pieces = len(cuts) - 1
    near_last = len(events) - 2
    turns = [near_last * hop // (chips - 1) for hop in range(1, chips)]

    def across(store):
        return lax.ppermute(store, "rep", ring)

    def turn(store):
        return lax.ppermute(store, "rep", swap)

    homes = block_home[replica_variant[rep]]
    holder = homes // slots
    away = (rep // CORES - holder // CORES + chips) % chips
    turned = (rep % CORES + holder % CORES) % CORES
    row_of = (turned * chips + away) * slots + homes % slots

    flight = [step(chain, 1) for chain in range(CHAINS)]
    deltas = pl.pallas_call(
        functools.partial(scale_kernel, block),
        out_shape=[
            jax.ShapeDtypeStruct(((high - low) * block, width), jnp.bfloat16)
            for low, high in zip(cuts[:-1], cuts[1:])
        ],
        in_specs=[SMEM, VMEM],
        out_specs=[VMEM] * pieces,
        compiler_params=pltpu.CompilerParams(vmem_limit_bytes=VMEM_LIMIT),
        cost_estimate=BRIEF,
    )(delta_scales.astype(jnp.float32), delta_codes)
    held, twins = [deltas], [[turn(delta) for delta in deltas]]
    sent = [across(delta) for delta in deltas]
    for index, (hop, chain) in enumerate(events[: near_last + 1]):
        rights[chain].append(flight[0][0])
        lefts[chain].append(flight[0][1])
        flight = flight[1:]
        if index in turns:
            taken = pieces if len(held) < chips - 1 else 1
            came, twins, rights, lefts = tie((sent[:taken], twins, rights, lefts))
        else:
            taken = 0
            rights, lefts = tie((rights, lefts))
        if hop + 1 < ranks:
            flight.append(step(chain, hop + 1))
        if taken:
            held.append(came)
            twins.append([turn(value) for value in came])
            sent = [across(value) for value in came] if taken == pieces else sent[1:]

    def merge(weight, chosen):
        parts, stores = [], []
        for core, kept in enumerate((held, twins)):
            for hop, piece in chosen:
                place = (core * chips + hop) * slots
                parts.append((place + cuts[piece], place + cuts[piece + 1]))
                stores.append(kept[hop][piece])
        inputs = [row_of, base_weight] + stores
        given = [] if weight is None else [weight]
        return pl.pallas_call(
            functools.partial(merge_kernel, block, tuple(parts)),
            out_shape=jax.ShapeDtypeStruct((depth, width), jnp.bfloat16),
            in_specs=[SMEM] + [HBM] * (1 + len(stores) + len(given)),
            out_specs=HBM,
            scratch_shapes=[
                pltpu.VMEM((depth, width), jnp.bfloat16),
                pltpu.VMEM((depth, width), jnp.bfloat16),
                pltpu.SemaphoreType.DMA((blocks,)),
                pltpu.SemaphoreType.DMA((blocks,)),
                pltpu.SemaphoreType.DMA((blocks,)),
            ],
            input_output_aliases={len(inputs): 0} if given else {},
            compiler_params=pltpu.CompilerParams(vmem_limit_bytes=VMEM_LIMIT),
            cost_estimate=BRIEF,
        )(*inputs, *given)

    there = [(hop, piece) for hop, values in enumerate(held) for piece in range(len(values))]
    weight = merge(None, there)
    sent, weight = tie((sent, weight))
    held[-1] = held[-1] + sent
    twins[-1] = twins[-1] + [turn(value) for value in sent]
    weight = merge(weight, [(chips - 1, piece) for piece in range(1, pieces)])
    flight, weight = tie((flight, weight))
    for (hop, chain), landing in zip(events[near_last + 1 :], flight):
        rights[chain].append(landing[0])
        lefts[chain].append(landing[1])

    arrays = []
    for chain in range(CHAINS):
        arrays += rights[chain] + lefts[chain][1:]
    total_rows = ranks * CHAINS * rows
    chunks = blocks // CHUNK_BLOCKS
    return pl.pallas_call(
        functools.partial(product_kernel, (ranks, CHUNK_BLOCKS * block)),
        out_shape=jax.ShapeDtypeStruct((total_rows, width), jnp.bfloat16),
        in_specs=[HBM] * (1 + len(arrays)),
        out_specs=VMEM,
        scratch_shapes=[
            pltpu.VMEM((total_rows, depth), jnp.bfloat16),
            pltpu.VMEM((depth, width), jnp.bfloat16),
            pltpu.VMEM((total_rows, width), jnp.float32),
            pltpu.SemaphoreType.DMA((chunks, CHAINS * ranks + 1)),
        ],
        compiler_params=pltpu.CompilerParams(vmem_limit_bytes=VMEM_LIMIT),
        cost_estimate=BRIEF,
    )(weight, *arrays)


def solution(mesh):
    in_specs = (
        P(("groups", "rep", "tp"), None),
        P(None, "tp"),
        P(("groups", "rep"), "tp"),
        P(("groups", "rep"), "tp"),
        P("groups"),
        P("groups", None),
    )
    out_specs = P(("groups", "rep"), "tp")
    return jax.shard_map(local, mesh=mesh, in_specs=in_specs, out_specs=out_specs, check_vma=False)
```

```python
import functools
import jax
import jax.numpy as jnp
from jax import lax
from jax.experimental import pallas as pl
from jax.experimental.pallas import tpu as pltpu
from jax.sharding import PartitionSpec as P

CORES = 2
CHUNK_BLOCKS = 8


CHAINS = 2
VMEM_LIMIT = 60 * 1024 * 1024
SMEM = pl.BlockSpec(memory_space=pltpu.SMEM)
VMEM = pl.BlockSpec(memory_space=pltpu.VMEM)
HBM = pl.BlockSpec(memory_space=pl.ANY)
BRIEF = pl.CostEstimate(flops=1, bytes_accessed=1, transcendentals=0)


def scale_kernel(block, edges, scale_ref, codes_ref, *out_refs):
    col_blocks = scale_ref.shape[1]
    wide = codes_ref.shape[1] // col_blocks
    count = codes_ref.shape[0] // block
    grid_step = pl.program_id(0)
    for out_ref, low, high in zip(out_refs, edges[:-1], edges[1:]):

        @pl.when((grid_step >= low) & (grid_step < high))
        def _():
            for index in range(count):
                rows = pl.ds(index * block, block)
                for col in range(col_blocks):
                    at = pl.ds(col * wide, wide)
                    delta = codes_ref[rows, at].astype(jnp.float32) * scale_ref[grid_step * count + index, col]
                    out_ref[rows, at] = delta.astype(jnp.bfloat16)


def merge_kernel(block, parts, row_ref, base_ref, *refs):
    stores = refs[: len(parts)]
    out_ref, base_buf, delta_buf, base_sems, delta_sems, out_sems = refs[-6:]
    blocks = row_ref.shape[0]

    def rows(index):
        return pl.ds(pl.multiple_of(index * block, block), block)

    def copies(index, store, slot):
        return (
            pltpu.make_async_copy(base_ref.at[rows(index), :], base_buf.at[rows(index), :], base_sems.at[index]),
            pltpu.make_async_copy(store.at[rows(slot), :], delta_buf.at[rows(index), :], delta_sems.at[index]),
        )

    def result(index):
        return pltpu.make_async_copy(base_buf.at[rows(index), :], out_ref.at[rows(index), :], out_sems.at[index])

    def inside(row, part):
        return (row >= part[0]) & (row < part[1])

    def present(index):
        row = row_ref[index]
        return functools.reduce(jnp.logical_or, [inside(row, part) for part in parts])

    @pl.loop(0, blocks)
    def _(index):
        row = row_ref[index]
        for part, store in zip(parts, stores):

            @pl.when(inside(row, part))
            def _():
                for copy in copies(index, store, row - part[0]):
                    copy.start()

    @pl.loop(0, blocks)
    def _(index):
        @pl.when(present(index))
        def _():
            for copy in copies(index, stores[0], 0):
                copy.wait()
            merged = base_buf[rows(index), :].astype(jnp.float32) + delta_buf[rows(index), :].astype(jnp.float32)
            base_buf[rows(index), :] = merged.astype(jnp.bfloat16)
            result(index).start()

    @pl.loop(0, blocks)
    def _(index):
        @pl.when(present(index))
        def _():
            result(index).wait()


def product_kernel(dims, weight_ref, *refs):
    ranks, joint, span = dims
    out_ref, token_buf, weight_buf, total, sems = refs[-5:]
    lanes = 2 * joint - 1
    half_refs = [refs[chain * lanes : (chain + 1) * lanes] for chain in range(CHAINS)]
    joint_refs = refs[CHAINS * lanes : -5]
    rows, depth = half_refs[0][0].shape
    chunks = depth // span
    rank = lax.axis_index("tp")

    def source(chain, hop, left):
        if hop >= joint:
            return joint_refs[hop - joint].at[pl.ds(chain * rows, rows), :]
        return half_refs[chain][hop + joint - 1 if left else hop]

    def weight_copy(chunk):
        at = pl.ds(pl.multiple_of(chunk * span, span), span)
        return pltpu.make_async_copy(weight_ref.at[at, :], weight_buf.at[at, :], sems.at[chunk, CHAINS * ranks])

    def token_copy(chunk, chain, hop, given):
        at = pl.ds(pl.multiple_of(chunk * span, span), span)
        origin = lax.rem(rank - hop + ranks, ranks)
        row = pl.multiple_of((origin * CHAINS + chain) * rows, rows)
        return pltpu.make_async_copy(
            given.at[:, at], token_buf.at[pl.ds(row, rows), at], sems.at[chunk, chain * ranks + hop]
        )

    @pl.loop(0, chunks)
    def _(chunk):
        weight_copy(chunk).start()
        for chain in range(CHAINS):
            token_copy(chunk, chain, 0, half_refs[chain][0]).start()
            for hop in range(1, ranks):
                from_left = rank >= hop

                @pl.when(from_left)
                def _():
                    token_copy(chunk, chain, hop, source(chain, hop, False)).start()

                @pl.when(jnp.logical_not(from_left))
                def _():
                    token_copy(chunk, chain, hop, source(chain, ranks - hop, True)).start()

    total[...] = jnp.zeros_like(total)

    @pl.loop(0, chunks)
    def _(chunk):
        weight_copy(chunk).wait()
        for chain in range(CHAINS):
            for hop in range(ranks):
                token_copy(chunk, chain, hop, half_refs[chain][0]).wait()
        at = pl.ds(pl.multiple_of(chunk * span, span), span)
        total[...] += jnp.dot(token_buf[:, at], weight_buf[at, :], preferred_element_type=jnp.float32)

    out_ref[...] = total[...].astype(out_ref.dtype)


def local(tokens, base_weight, delta_codes, delta_scales, replica_variant, block_home):
    ranks, reps = lax.axis_size("tp"), lax.axis_size("rep")
    blocks = block_home.shape[1]
    depth, width = base_weight.shape
    rows = tokens.shape[0] // CHAINS
    block = depth // blocks
    slots = delta_scales.shape[0]
    rep = lax.axis_index("rep")
    chips = reps // CORES
    ring = [(i, (i + CORES) % reps) for i in range(reps)]
    swap = [(i, i // CORES * CORES + (i + 1) % CORES) for i in range(reps)]

    def tie(values):
        return lax.optimization_barrier(values)

    def right(value, hop):
        return lax.ppermute(value, "tp", [(i, i + 1) for i in range(hop - 1, ranks - 1)])

    def left(value, hop):
        return lax.ppermute(value, "tp", [(i, i - 1) for i in range(1, ranks - hop + 1)])

    def step(chain, hop):
        return right(rights[chain][-1], hop), left(lefts[chain][-1], hop)

    halves = [tokens[chain * rows : (chain + 1) * rows] for chain in range(CHAINS)]
    rights, lefts = [[half] for half in halves], [[half] for half in halves]
    joint = ranks // 2 + 1
    events = [(hop, chain) for hop in range(1, joint) for chain in range(CHAINS)]
    most = slots * 3 // 4
    cuts = [0, most, slots]
    pieces = len(cuts) - 1
    near_last = len(events) - 1
    turns = [near_last * hop // (chips - 1) for hop in range(1, chips)]

    def across(store):
        return lax.ppermute(store, "rep", ring)

    def turn(store):
        return lax.ppermute(store, "rep", swap)

    homes = block_home[replica_variant[rep]]
    holder = homes // slots
    away = (rep // CORES - holder // CORES + chips) % chips
    turned = (rep % CORES + holder % CORES) % CORES
    row_of = (turned * chips + away) * slots + homes % slots

    flight = [step(chain, 1) for chain in range(CHAINS)]
    count = slots // 8
    edges = [cut // count for cut in cuts]

    def piece_spec(low, high):
        return pl.BlockSpec((count * block, width), lambda i: (jnp.clip(i, low, high - 1) - low, 0))

    deltas = pl.pallas_call(
        functools.partial(scale_kernel, block, tuple(edges)),
        grid=(slots // count,),
        out_shape=[
            jax.ShapeDtypeStruct(((high - low) * block, width), jnp.bfloat16)
            for low, high in zip(cuts[:-1], cuts[1:])
        ],
        in_specs=[SMEM, pl.BlockSpec((count * block, width), lambda i: (i, 0))],
        out_specs=[piece_spec(low, high) for low, high in zip(edges[:-1], edges[1:])],
        compiler_params=pltpu.CompilerParams(vmem_limit_bytes=VMEM_LIMIT),
        cost_estimate=BRIEF,
    )(delta_scales.astype(jnp.float32), delta_codes)
    held, twins = [deltas], [[turn(delta) for delta in deltas]]
    sent = [across(delta) for delta in deltas]
    for index, (hop, chain) in enumerate(events[: near_last + 1]):
        rights[chain].append(flight[0][0])
        lefts[chain].append(flight[0][1])
        flight = flight[1:]
        if index in turns:
            taken = pieces if len(held) < chips - 1 else 1
            came, twins, rights, lefts = tie((sent[:taken], twins, rights, lefts))
        else:
            taken = 0
            rights, lefts = tie((rights, lefts))
        if hop + 1 < joint:
            flight.append(step(chain, hop + 1))
        if taken:
            held.append(came)
            twins.append([turn(value) for value in came])
            sent = [across(value) for value in came] if taken == pieces else sent[1:]

    pairs = [
        [(i, i + 1) for i in range(hop - 1, ranks - 1)] + [(i, i - 1) for i in range(1, ranks - hop + 1)]
        for hop in range(joint, ranks)
    ]
    from_left = lax.axis_index("tp") >= joint - 1
    whole = jnp.where(
        from_left,
        jnp.concatenate([values[-1] for values in rights], axis=0),
        jnp.concatenate([values[-1] for values in lefts], axis=0),
    )
    whole_steps = []
    for pair in pairs:
        whole = lax.ppermute(whole, "tp", pair)
        whole_steps.append(whole)

    def merge(weight, chosen):
        parts, stores = [], []
        for core, kept in enumerate((held, twins)):
            for hop, piece in chosen:
                place = (core * chips + hop) * slots
                parts.append((place + cuts[piece], place + cuts[piece + 1]))
                stores.append(kept[hop][piece])
        inputs = [row_of, base_weight] + stores
        given = [] if weight is None else [weight]
        return pl.pallas_call(
            functools.partial(merge_kernel, block, tuple(parts)),
            out_shape=jax.ShapeDtypeStruct((depth, width), jnp.bfloat16),
            in_specs=[SMEM] + [HBM] * (1 + len(stores) + len(given)),
            out_specs=HBM,
            scratch_shapes=[
                pltpu.VMEM((depth, width), jnp.bfloat16),
                pltpu.VMEM((depth, width), jnp.bfloat16),
                pltpu.SemaphoreType.DMA((blocks,)),
                pltpu.SemaphoreType.DMA((blocks,)),
                pltpu.SemaphoreType.DMA((blocks,)),
            ],
            input_output_aliases={len(inputs): 0} if given else {},
            compiler_params=pltpu.CompilerParams(vmem_limit_bytes=VMEM_LIMIT),
            cost_estimate=BRIEF,
        )(*inputs, *given)

    there = [(hop, piece) for hop, values in enumerate(held) for piece in range(len(values))]
    weight = merge(None, there)
    sent, weight = tie((sent, weight))
    held[-1] = held[-1] + sent
    twins[-1] = twins[-1] + [turn(value) for value in sent]
    weight = merge(weight, [(chips - 1, piece) for piece in range(1, pieces)])
    whole_steps, weight = tie((whole_steps, weight))
    arrays = []
    for chain in range(CHAINS):
        arrays += rights[chain] + lefts[chain][1:]
    arrays += whole_steps
    total_rows = ranks * CHAINS * rows
    chunks = blocks // CHUNK_BLOCKS
    return pl.pallas_call(
        functools.partial(product_kernel, (ranks, joint, CHUNK_BLOCKS * block)),
        out_shape=jax.ShapeDtypeStruct((total_rows, width), jnp.bfloat16),
        in_specs=[HBM] * (1 + len(arrays)),
        out_specs=VMEM,
        scratch_shapes=[
            pltpu.VMEM((total_rows, depth), jnp.bfloat16),
            pltpu.VMEM((depth, width), jnp.bfloat16),
            pltpu.VMEM((total_rows, width), jnp.float32),
            pltpu.SemaphoreType.DMA((chunks, CHAINS * ranks + 1)),
        ],
        compiler_params=pltpu.CompilerParams(vmem_limit_bytes=VMEM_LIMIT),
        cost_estimate=BRIEF,
    )(weight, *arrays)


def solution(mesh):
    in_specs = (
        P(("groups", "rep", "tp"), None),
        P(None, "tp"),
        P(("groups", "rep"), "tp"),
        P(("groups", "rep"), "tp"),
        P("groups"),
        P("groups", None),
    )
    out_specs = P(("groups", "rep"), "tp")
    return jax.shard_map(local, mesh=mesh, in_specs=in_specs, out_specs=out_specs, check_vma=False)
```

```python
import functools
import jax
import jax.numpy as jnp
from jax import lax
from jax.experimental import pallas as pl
from jax.experimental.pallas import tpu as pltpu
from jax.sharding import PartitionSpec as P

CORES = 2
CHUNK_BLOCKS = 8


VMEM_LIMIT = 60 * 1024 * 1024
SMEM = pl.BlockSpec(memory_space=pltpu.SMEM)
VMEM = pl.BlockSpec(memory_space=pltpu.VMEM)
HBM = pl.BlockSpec(memory_space=pl.ANY)
BRIEF = pl.CostEstimate(flops=1, bytes_accessed=1, transcendentals=0)


def scale_kernel(block, scale_ref, codes_ref, *out_refs):
    col_blocks = scale_ref.shape[1]
    wide = codes_ref.shape[1] // col_blocks
    first = 0
    for out_ref in out_refs:
        count = out_ref.shape[0] // block

        @pl.loop(0, count)
        def _(index):
            source = pl.ds(pl.multiple_of((first + index) * block, block), block)
            target = pl.ds(pl.multiple_of(index * block, block), block)
            for col in range(col_blocks):
                at = pl.ds(col * wide, wide)
                delta = codes_ref[source, at].astype(jnp.float32) * scale_ref[first + index, col]
                out_ref[target, at] = delta.astype(jnp.bfloat16)

        first += count


def merge_kernel(block, parts, block_ref, base_ref, *refs):
    stores = refs[: len(parts)]
    out_ref, base_buf, delta_buf, base_sems, delta_sems, out_sems = refs[-6:]

    def rows(index):
        return pl.ds(pl.multiple_of(index * block, block), block)

    def copies(index, store, slot):
        return (
            pltpu.make_async_copy(base_ref.at[rows(index), :], base_buf.at[rows(index), :], base_sems.at[index]),
            pltpu.make_async_copy(store.at[rows(slot), :], delta_buf.at[rows(index), :], delta_sems.at[index]),
        )

    def result(index):
        return pltpu.make_async_copy(base_buf.at[rows(index), :], out_ref.at[rows(index), :], out_sems.at[index])

    def each(visit):
        for (low, high), store in zip(parts, stores):

            @pl.loop(low, high)
            def _(row):
                index = block_ref[row]

                @pl.when(index >= 0)
                def _():
                    visit(index, store, row - low)

    def fetch(index, store, slot):
        for copy in copies(index, store, slot):
            copy.start()

    def merge(index, store, slot):
        for copy in copies(index, store, slot):
            copy.wait()
        merged = base_buf[rows(index), :].astype(jnp.float32) + delta_buf[rows(index), :].astype(jnp.float32)
        base_buf[rows(index), :] = merged.astype(jnp.bfloat16)
        result(index).start()

    each(fetch)
    each(merge)
    each(lambda index, store, slot: result(index).wait())


def product_kernel(dims, weight_ref, *refs):
    ranks, span, last = dims
    given = 2 * ranks - 1 if last else 2 * ranks - 3
    own, rights = refs[0], refs[1 : (given + 1) // 2]
    lefts = refs[(given + 1) // 2 : given]
    out_ref, token_buf, weight_buf, total, sems = refs[-5:] if not last else refs[-6:-1]
    rows, depth = own.shape
    chunks = depth // span
    rank = lax.axis_index("tp")
    star = lax.rem(2 * rank + 1, ranks)

    def columns(chunk):
        return pl.ds(pl.multiple_of(chunk * span, span), span)

    def origin_rows(hop):
        return pl.ds(pl.multiple_of(lax.rem(rank - hop + ranks, ranks) * rows, rows), rows)

    def slot_rows(hop):
        slot = 0 if last else hop - (star < hop).astype(jnp.int32)
        return pl.ds(pl.multiple_of(slot * rows, rows), rows)

    def weight_copy(chunk):
        at = columns(chunk)
        return pltpu.make_async_copy(weight_ref.at[at, :], weight_buf.at[at, :], sems.at[chunk, ranks])

    def token_copy(chunk, hop, source):
        at = columns(chunk)
        return pltpu.make_async_copy(source.at[:, at], token_buf.at[slot_rows(hop), at], sems.at[chunk, hop])

    def each(visit):
        for hop in range(ranks):

            @pl.when((star == hop) if last else (star != hop))
            def _():
                visit(hop)

    def fetch(chunk, hop):
        if hop == 0:
            token_copy(chunk, hop, own).start()
            return
        if hop <= len(rights):

            @pl.when(rank >= hop)
            def _():
                token_copy(chunk, hop, rights[hop - 1]).start()

        if ranks - hop <= len(lefts):

            @pl.when(rank < hop)
            def _():
                token_copy(chunk, hop, lefts[ranks - hop - 1]).start()

    @pl.loop(0, chunks)
    def _(chunk):
        weight_copy(chunk).start()
        each(functools.partial(fetch, chunk))

    total[...] = jnp.zeros_like(total)

    @pl.loop(0, chunks)
    def _(chunk):
        weight_copy(chunk).wait()
        each(lambda hop: token_copy(chunk, hop, own).wait())
        at = columns(chunk)
        total[...] += jnp.dot(token_buf[:, at], weight_buf[at, :], preferred_element_type=jnp.float32)

    if last:
        result = refs[-1]
        result[...] = total[...].astype(result.dtype)

        def store(hop):
            pltpu.sync_copy(result, out_ref.at[origin_rows(hop), :])

    else:

        def store(hop):
            out_ref[origin_rows(hop), :] = total[slot_rows(hop), :].astype(out_ref.dtype)

    each(store)


def local(tokens, base_weight, delta_codes, delta_scales, replica_variant, block_home):
    ranks, reps = lax.axis_size("tp"), lax.axis_size("rep")
    blocks = block_home.shape[1]
    depth, width = base_weight.shape
    rows = tokens.shape[0]
    block = depth // blocks
    slots = delta_scales.shape[0]
    rep = lax.axis_index("rep")
    chips = reps // CORES
    ring = [(i, (i + CORES) % reps) for i in range(reps)]
    swap = [(i, i // CORES * CORES + (i + 1) % CORES) for i in range(reps)]

    def tie(values):
        return lax.optimization_barrier(values)

    def right(value, hop):
        return lax.ppermute(value, "tp", [(i, i + 1) for i in range(hop - 1, ranks - 1)])

    def left(value, hop):
        return lax.ppermute(value, "tp", [(i, i - 1) for i in range(1, ranks - hop + 1)])

    rights, lefts = [tokens], [tokens]
    cuts = [0, slots * 3 // 4, slots]
    pieces = len(cuts) - 1

    def across(store):
        return lax.ppermute(store, "rep", ring)

    def turn(store):
        return lax.ppermute(store, "rep", swap)

    homes = block_home[replica_variant[rep]]
    holder = homes // slots
    away = (rep // CORES - holder // CORES + chips) % chips
    turned = (rep % CORES + holder % CORES) % CORES
    row_of = (turned * chips + away) * slots + homes % slots
    here = row_of[None, :] == jnp.arange(reps * slots, dtype=jnp.int32)[:, None]
    block_of = jnp.max(jnp.where(here, jnp.arange(blocks, dtype=jnp.int32)[None, :], -1), axis=1)

    deltas = pl.pallas_call(
        functools.partial(scale_kernel, block),
        out_shape=[
            jax.ShapeDtypeStruct(((high - low) * block, width), jnp.bfloat16)
            for low, high in zip(cuts[:-1], cuts[1:])
        ],
        in_specs=[SMEM, VMEM],
        out_specs=[VMEM] * pieces,
        compiler_params=pltpu.CompilerParams(vmem_limit_bytes=VMEM_LIMIT),
        cost_estimate=BRIEF,
    )(delta_scales.astype(jnp.float32), delta_codes)
    held, twins = [deltas], [[turn(delta) for delta in deltas]]
    sent = [across(delta) for delta in deltas]
    turns = [(ranks - 2) * hop // (chips - 1) for hop in range(1, chips)]
    for hop in range(1, ranks):
        came_right, came_left = right(rights[-1], hop), left(lefts[-1], hop)
        if hop == ranks - 1:
            break
        taken = 0
        if hop in turns:
            taken = pieces if len(held) < chips - 1 else 1
        if taken:
            came, twins, came_right, came_left = tie((sent[:taken], twins, came_right, came_left))
        else:
            came_right, came_left = tie((came_right, came_left))
        rights.append(came_right)
        lefts.append(came_left)
        if taken:
            held.append(came)
            twins.append([turn(value) for value in came])
            sent = [across(value) for value in came] if taken == pieces else sent[taken:]

    def merge(weight, chosen):
        parts, stores = [], []
        for core, kept in enumerate((held, twins)):
            for hop, piece in chosen:
                place = (core * chips + hop) * slots
                parts.append((place + cuts[piece], place + cuts[piece + 1]))
                stores.append(kept[hop][piece])
        inputs = [block_of, base_weight] + stores
        given = [] if weight is None else [weight]
        return pl.pallas_call(
            functools.partial(merge_kernel, block, tuple(parts)),
            out_shape=jax.ShapeDtypeStruct((depth, width), jnp.bfloat16),
            in_specs=[SMEM] + [HBM] * (1 + len(stores) + len(given)),
            out_specs=HBM,
            scratch_shapes=[
                pltpu.VMEM((depth, width), jnp.bfloat16),
                pltpu.VMEM((depth, width), jnp.bfloat16),
                pltpu.SemaphoreType.DMA((blocks,)),
                pltpu.SemaphoreType.DMA((blocks,)),
                pltpu.SemaphoreType.DMA((blocks,)),
            ],
            input_output_aliases={len(inputs): 0} if given else {},
            compiler_params=pltpu.CompilerParams(vmem_limit_bytes=VMEM_LIMIT),
            cost_estimate=BRIEF,
        )(*inputs, *given)

    there = [(hop, piece) for hop, values in enumerate(held) for piece in range(len(values))]
    weight = merge(None, there)
    sent, weight = tie((sent, weight))
    held[-1] = held[-1] + sent
    twins[-1] = twins[-1] + [turn(value) for value in sent]
    weight = merge(weight, [(chips - 1, piece) for piece in range(1, pieces)])
    chunks = blocks // CHUNK_BLOCKS

    def product(arrays, prior):
        last = prior is not None
        count = 1 if last else ranks - 1
        inputs = [weight] + arrays + ([prior] if last else [])
        scratch = [
            pltpu.VMEM((count * rows, depth), jnp.bfloat16),
            pltpu.VMEM((depth, width), jnp.bfloat16),
            pltpu.VMEM((count * rows, width), jnp.float32),
            pltpu.SemaphoreType.DMA((chunks, ranks + 1)),
        ]
        return pl.pallas_call(
            functools.partial(product_kernel, (ranks, CHUNK_BLOCKS * block, last)),
            out_shape=jax.ShapeDtypeStruct((ranks * rows, width), jnp.bfloat16),
            in_specs=[HBM] * len(inputs),
            out_specs=HBM if last else VMEM,
            scratch_shapes=scratch + ([pltpu.VMEM((rows, width), jnp.bfloat16)] if last else []),
            input_output_aliases={len(inputs) - 1: 0} if last else {},
            compiler_params=pltpu.CompilerParams(vmem_limit_bytes=VMEM_LIMIT),
            cost_estimate=BRIEF,
        )(*inputs)

    early = product(rights + lefts[1:], None)
    (came_right, came_left), early = tie(((came_right, came_left), early))
    return product(rights + [came_right] + lefts[1:] + [came_left], early)


def solution(mesh):
    in_specs = (
        P(("groups", "rep", "tp"), None),
        P(None, "tp"),
        P(("groups", "rep"), "tp"),
        P(("groups", "rep"), "tp"),
        P("groups"),
        P("groups", None),
    )
    out_specs = P(("groups", "rep"), "tp")
    return jax.shard_map(local, mesh=mesh, in_specs=in_specs, out_specs=out_specs, check_vma=False)
```

```python
import functools
import jax
import jax.numpy as jnp
from jax import lax
from jax.experimental import pallas as pl
from jax.experimental.pallas import tpu as pltpu
from jax.sharding import PartitionSpec as P

CORES = 2
CHUNK_BLOCKS = 8


VMEM_LIMIT = 60 * 1024 * 1024
SMEM = pl.BlockSpec(memory_space=pltpu.SMEM)
VMEM = pl.BlockSpec(memory_space=pltpu.VMEM)
HBM = pl.BlockSpec(memory_space=pl.ANY)
BRIEF = pl.CostEstimate(flops=1, bytes_accessed=1, transcendentals=0)


def scale_kernel(block, scale_ref, codes_ref, *out_refs):
    col_blocks = scale_ref.shape[1]
    wide = codes_ref.shape[1] // col_blocks
    first = 0
    for out_ref in out_refs:
        count = out_ref.shape[0] // block

        @pl.loop(0, count)
        def _(index):
            source = pl.ds(pl.multiple_of((first + index) * block, block), block)
            target = pl.ds(pl.multiple_of(index * block, block), block)
            for col in range(col_blocks):
                at = pl.ds(col * wide, wide)
                delta = codes_ref[source, at].astype(jnp.float32) * scale_ref[first + index, col]
                out_ref[target, at] = delta.astype(jnp.bfloat16)

        first += count


def merge_kernel(block, parts, block_ref, base_ref, *refs):
    stores = refs[: len(parts)]
    out_ref, base_buf, delta_buf, base_sems, delta_sems, out_sems = refs[-6:]

    def rows(index):
        return pl.ds(pl.multiple_of(index * block, block), block)

    def copies(index, store, slot):
        return (
            pltpu.make_async_copy(base_ref.at[rows(index), :], base_buf.at[rows(index), :], base_sems.at[index]),
            pltpu.make_async_copy(store.at[rows(slot), :], delta_buf.at[rows(index), :], delta_sems.at[index]),
        )

    def result(index):
        return pltpu.make_async_copy(base_buf.at[rows(index), :], out_ref.at[rows(index), :], out_sems.at[index])

    def each(visit):
        for (low, high), store in zip(parts, stores):

            @pl.loop(low, high)
            def _(row):
                index = block_ref[row]

                @pl.when(index >= 0)
                def _():
                    visit(index, store, row - low)

    def fetch(index, store, slot):
        for copy in copies(index, store, slot):
            copy.start()

    def merge(index, store, slot):
        for copy in copies(index, store, slot):
            copy.wait()
        merged = base_buf[rows(index), :].astype(jnp.float32) + delta_buf[rows(index), :].astype(jnp.float32)
        base_buf[rows(index), :] = merged.astype(jnp.bfloat16)
        result(index).start()

    each(fetch)
    each(merge)
    each(lambda index, store, slot: result(index).wait())


def product_kernel(dims, weight_ref, *refs):
    ranks, span, last = dims
    given = 2 * ranks - 1 if last else 2 * ranks - 3
    own, rights = refs[0], refs[1 : (given + 1) // 2]
    lefts = refs[(given + 1) // 2 : given]
    out_ref, token_buf, weight_buf, total, sems = refs[-5:] if not last else refs[-6:-1]
    rows, depth = own.shape
    chunks = depth // span
    rank = lax.axis_index("tp")
    star = lax.rem(2 * rank + 1, ranks)

    def columns(chunk):
        return pl.ds(pl.multiple_of(chunk * span, span), span)

    def origin_rows(hop):
        return pl.ds(pl.multiple_of(lax.rem(rank - hop + ranks, ranks) * rows, rows), rows)

    def slot_rows(hop):
        slot = 0 if last else hop - (star < hop).astype(jnp.int32)
        return pl.ds(pl.multiple_of(slot * rows, rows), rows)

    def weight_copy(chunk):
        at = columns(chunk)
        return pltpu.make_async_copy(weight_ref.at[at, :], weight_buf.at[at, :], sems.at[chunk, ranks])

    def token_copy(chunk, hop, source):
        at = columns(chunk)
        return pltpu.make_async_copy(source.at[:, at], token_buf.at[slot_rows(hop), at], sems.at[chunk, hop])

    def each(visit):
        for hop in range(ranks):

            @pl.when((star == hop) if last else (star != hop))
            def _():
                visit(hop)

    def fetch(chunk, hop):
        if hop == 0:
            token_copy(chunk, hop, own).start()
            return
        if hop <= len(rights):

            @pl.when(rank >= hop)
            def _():
                token_copy(chunk, hop, rights[hop - 1]).start()

        if ranks - hop <= len(lefts):

            @pl.when(rank < hop)
            def _():
                token_copy(chunk, hop, lefts[ranks - hop - 1]).start()

    @pl.loop(0, chunks)
    def _(chunk):
        weight_copy(chunk).start()
        each(functools.partial(fetch, chunk))

    total[...] = jnp.zeros_like(total)

    @pl.loop(0, chunks)
    def _(chunk):
        weight_copy(chunk).wait()
        each(lambda hop: token_copy(chunk, hop, own).wait())
        at = columns(chunk)
        total[...] += jnp.dot(token_buf[:, at], weight_buf[at, :], preferred_element_type=jnp.float32)

    if last:
        result = refs[-1]
        result[...] = total[...].astype(result.dtype)

        def store(hop):
            pltpu.sync_copy(result, out_ref.at[origin_rows(hop), :])

    else:

        def store(hop):
            out_ref[origin_rows(hop), :] = total[slot_rows(hop), :].astype(out_ref.dtype)

    each(store)


def local(tokens, base_weight, delta_codes, delta_scales, replica_variant, block_home):
    ranks, reps = lax.axis_size("tp"), lax.axis_size("rep")
    blocks = block_home.shape[1]
    depth, width = base_weight.shape
    rows = tokens.shape[0]
    block = depth // blocks
    slots = delta_scales.shape[0]
    rep = lax.axis_index("rep")
    chips = reps // CORES
    ring = [(i, (i + CORES) % reps) for i in range(reps)]
    swap = [(i, i // CORES * CORES + (i + 1) % CORES) for i in range(reps)]

    def tie(values):
        return lax.optimization_barrier(values)

    def right(value, hop):
        return lax.ppermute(value, "tp", [(i, i + 1) for i in range(hop - 1, ranks - 1)])

    def left(value, hop):
        return lax.ppermute(value, "tp", [(i, i - 1) for i in range(1, ranks - hop + 1)])

    rights, lefts = [tokens], [tokens]
    cuts = [-(-slots * i // 3) for i in range(4)]
    pieces = len(cuts) - 1

    def across(store):
        return lax.ppermute(store, "rep", ring)

    def turn(store):
        return lax.ppermute(store, "rep", swap)

    homes = block_home[replica_variant[rep]]
    holder = homes // slots
    away = (rep // CORES - holder // CORES + chips) % chips
    turned = (rep % CORES + holder % CORES) % CORES
    row_of = (turned * chips + away) * slots + homes % slots
    here = row_of[None, :] == jnp.arange(reps * slots, dtype=jnp.int32)[:, None]
    block_of = jnp.max(jnp.where(here, jnp.arange(blocks, dtype=jnp.int32)[None, :], -1), axis=1)

    deltas = pl.pallas_call(
        functools.partial(scale_kernel, block),
        out_shape=[
            jax.ShapeDtypeStruct(((high - low) * block, width), jnp.bfloat16)
            for low, high in zip(cuts[:-1], cuts[1:])
        ],
        in_specs=[SMEM, VMEM],
        out_specs=[VMEM] * pieces,
        compiler_params=pltpu.CompilerParams(vmem_limit_bytes=VMEM_LIMIT),
        cost_estimate=BRIEF,
    )(delta_scales.astype(jnp.float32), delta_codes)
    held = [deltas] + [[] for _ in range(1, chips)]
    twins = [[turn(delta) for delta in deltas]] + [[] for _ in range(1, chips)]
    moves = [(hop, piece) for hop in range(1, chips) for piece in range(pieces)]
    flying = {(1, piece): across(delta) for piece, delta in enumerate(deltas)}

    def take(move, value):
        hop, piece = move
        held[hop].append(value)
        twins[hop].append(turn(value))
        if hop + 1 < chips:
            flying[hop + 1, piece] = across(value)

    done = 0
    for hop in range(1, ranks):
        came_right, came_left = right(rights[-1], hop), left(lefts[-1], hop)
        if hop == ranks - 1:
            break
        batch = moves[done : (len(moves) - 1) * hop // (ranks - 2)]
        came = [flying.pop(move) for move in batch]
        done += len(batch)
        came, came_right, came_left = tie((came, came_right, came_left))
        if hop == ranks - 2:
            twins[0], came_right, came_left = tie((twins[0], came_right, came_left))
        rights.append(came_right)
        lefts.append(came_left)
        for move, value in zip(batch, came):
            take(move, value)

    def merge(weight, chosen):
        parts, stores = [], []
        for core, kept in enumerate((held, twins)):
            for hop, piece in chosen:
                place = (core * chips + hop) * slots
                parts.append((place + cuts[piece], place + cuts[piece + 1]))
                stores.append(kept[hop][piece])
        inputs = [block_of, base_weight] + stores
        given = [] if weight is None else [weight]
        return pl.pallas_call(
            functools.partial(merge_kernel, block, tuple(parts)),
            out_shape=jax.ShapeDtypeStruct((depth, width), jnp.bfloat16),
            in_specs=[SMEM] + [HBM] * (1 + len(stores) + len(given)),
            out_specs=HBM,
            scratch_shapes=[
                pltpu.VMEM((depth, width), jnp.bfloat16),
                pltpu.VMEM((depth, width), jnp.bfloat16),
                pltpu.SemaphoreType.DMA((blocks,)),
                pltpu.SemaphoreType.DMA((blocks,)),
                pltpu.SemaphoreType.DMA((blocks,)),
            ],
            input_output_aliases={len(inputs): 0} if given else {},
            compiler_params=pltpu.CompilerParams(vmem_limit_bytes=VMEM_LIMIT),
            cost_estimate=BRIEF,
        )(*inputs, *given)

    weight = merge(None, [(hop, piece) for hop in range(chips) for piece in range(len(held[hop]))])
    came, weight = tie((flying.pop(moves[-1]), weight))
    take(moves[-1], came)
    weight = merge(weight, moves[-1:])
    chunks = blocks // CHUNK_BLOCKS

    def product(arrays, prior):
        last = prior is not None
        count = 1 if last else ranks - 1
        inputs = [weight] + arrays + ([prior] if last else [])
        scratch = [
            pltpu.VMEM((count * rows, depth), jnp.bfloat16),
            pltpu.VMEM((depth, width), jnp.bfloat16),
            pltpu.VMEM((count * rows, width), jnp.float32),
            pltpu.SemaphoreType.DMA((chunks, ranks + 1)),
        ]
        return pl.pallas_call(
            functools.partial(product_kernel, (ranks, CHUNK_BLOCKS * block, last)),
            out_shape=jax.ShapeDtypeStruct((ranks * rows, width), jnp.bfloat16),
            in_specs=[HBM] * len(inputs),
            out_specs=HBM if last else VMEM,
            scratch_shapes=scratch + ([pltpu.VMEM((rows, width), jnp.bfloat16)] if last else []),
            input_output_aliases={len(inputs) - 1: 0} if last else {},
            compiler_params=pltpu.CompilerParams(vmem_limit_bytes=VMEM_LIMIT),
            cost_estimate=BRIEF,
        )(*inputs)

    early = product(rights + lefts[1:], None)
    (came_right, came_left), early = tie(((came_right, came_left), early))
    return product(rights + [came_right] + lefts[1:] + [came_left], early)


def solution(mesh):
    in_specs = (
        P(("groups", "rep", "tp"), None),
        P(None, "tp"),
        P(("groups", "rep"), "tp"),
        P(("groups", "rep"), "tp"),
        P("groups"),
        P("groups", None),
    )
    out_specs = P(("groups", "rep"), "tp")
    return jax.shard_map(local, mesh=mesh, in_specs=in_specs, out_specs=out_specs, check_vma=False)
```

```python
import functools
import jax
import jax.numpy as jnp
from jax import lax
from jax.experimental import pallas as pl
from jax.experimental.pallas import tpu as pltpu
from jax.sharding import PartitionSpec as P

CORES = 2
CHUNK_BLOCKS = 8


ALL, EARLY, LAST = 0, 1, 2
VMEM_LIMIT = 60 * 1024 * 1024
SMEM = pl.BlockSpec(memory_space=pltpu.SMEM)
VMEM = pl.BlockSpec(memory_space=pltpu.VMEM)
HBM = pl.BlockSpec(memory_space=pl.ANY)
BRIEF = pl.CostEstimate(flops=1, bytes_accessed=1, transcendentals=0)


def scale_kernel(block, scale_ref, codes_ref, *out_refs):
    col_blocks = scale_ref.shape[1]
    wide = codes_ref.shape[1] // col_blocks
    first = 0
    for out_ref in out_refs:
        count = out_ref.shape[0] // block

        @pl.loop(0, count)
        def _(index):
            source = pl.ds(pl.multiple_of((first + index) * block, block), block)
            target = pl.ds(pl.multiple_of(index * block, block), block)
            for col in range(col_blocks):
                at = pl.ds(col * wide, wide)
                delta = codes_ref[source, at].astype(jnp.float32) * scale_ref[first + index, col]
                out_ref[target, at] = delta.astype(jnp.bfloat16)

        first += count


def merge_kernel(block, parts, block_ref, base_ref, *refs):
    stores = refs[: len(parts)]
    out_ref, base_buf, delta_buf, base_sems, delta_sems, out_sems = refs[-6:]

    def rows(index):
        return pl.ds(pl.multiple_of(index * block, block), block)

    def copies(index, store, slot):
        return (
            pltpu.make_async_copy(base_ref.at[rows(index), :], base_buf.at[rows(index), :], base_sems.at[index]),
            pltpu.make_async_copy(store.at[rows(slot), :], delta_buf.at[rows(index), :], delta_sems.at[index]),
        )

    def result(index):
        return pltpu.make_async_copy(base_buf.at[rows(index), :], out_ref.at[rows(index), :], out_sems.at[index])

    def each(visit):
        for (low, high), store in zip(parts, stores):

            @pl.loop(low, high)
            def _(row):
                index = block_ref[row]

                @pl.when(index >= 0)
                def _():
                    visit(index, store, row - low)

    def fetch(index, store, slot):
        for copy in copies(index, store, slot):
            copy.start()

    def merge(index, store, slot):
        for copy in copies(index, store, slot):
            copy.wait()
        merged = base_buf[rows(index), :].astype(jnp.float32) + delta_buf[rows(index), :].astype(jnp.float32)
        base_buf[rows(index), :] = merged.astype(jnp.bfloat16)
        result(index).start()

    each(fetch)
    each(merge)
    each(lambda index, store, slot: result(index).wait())


def product_kernel(dims, weight_ref, *refs):
    ranks, span, which = dims
    last = which == LAST
    given = 2 * ranks - 3 if which == EARLY else 2 * ranks - 1
    own, rights = refs[0], refs[1 : (given + 1) // 2]
    lefts = refs[(given + 1) // 2 : given]
    out_ref, token_buf, weight_buf, total, sems = refs[-5:] if not last else refs[-6:-1]
    rows, depth = own.shape
    chunks = depth // span
    rank = lax.axis_index("tp")
    star = lax.rem(2 * rank + 1, ranks)

    def columns(chunk):
        return pl.ds(pl.multiple_of(chunk * span, span), span)

    def origin_rows(hop):
        return pl.ds(pl.multiple_of(lax.rem(rank - hop + ranks, ranks) * rows, rows), rows)

    def slot_rows(hop):
        slot = {ALL: hop, EARLY: hop - (star < hop).astype(jnp.int32), LAST: 0}[which]
        return pl.ds(pl.multiple_of(slot * rows, rows), rows)

    def weight_copy(chunk):
        at = columns(chunk)
        return pltpu.make_async_copy(weight_ref.at[at, :], weight_buf.at[at, :], sems.at[chunk, ranks])

    def token_copy(chunk, hop, source):
        at = columns(chunk)
        return pltpu.make_async_copy(source.at[:, at], token_buf.at[slot_rows(hop), at], sems.at[chunk, hop])

    def each(visit):
        for hop in range(ranks):

            @pl.when({ALL: hop >= 0, EARLY: star != hop, LAST: star == hop}[which])
            def _():
                visit(hop)

    def fetch(chunk, hop):
        if hop == 0:
            token_copy(chunk, hop, own).start()
            return
        if hop <= len(rights):

            @pl.when(rank >= hop)
            def _():
                token_copy(chunk, hop, rights[hop - 1]).start()

        if ranks - hop <= len(lefts):

            @pl.when(rank < hop)
            def _():
                token_copy(chunk, hop, lefts[ranks - hop - 1]).start()

    @pl.loop(0, chunks)
    def _(chunk):
        weight_copy(chunk).start()
        each(functools.partial(fetch, chunk))

    total[...] = jnp.zeros_like(total)

    @pl.loop(0, chunks)
    def _(chunk):
        weight_copy(chunk).wait()
        each(lambda hop: token_copy(chunk, hop, own).wait())
        at = columns(chunk)
        total[...] += jnp.dot(token_buf[:, at], weight_buf[at, :], preferred_element_type=jnp.float32)

    if last:
        result = refs[-1]
        result[...] = total[...].astype(result.dtype)

        def store(hop):
            pltpu.sync_copy(result, out_ref.at[origin_rows(hop), :])

    else:

        def store(hop):
            out_ref[origin_rows(hop), :] = total[slot_rows(hop), :].astype(out_ref.dtype)

    each(store)


def local(tokens, base_weight, delta_codes, delta_scales, replica_variant, block_home):
    ranks, reps = lax.axis_size("tp"), lax.axis_size("rep")
    blocks = block_home.shape[1]
    depth, width = base_weight.shape
    rows = tokens.shape[0]
    block = depth // blocks
    slots = delta_scales.shape[0]
    rep = lax.axis_index("rep")
    chips = reps // CORES
    ring = [(i, (i + CORES) % reps) for i in range(reps)]
    swap = [(i, i // CORES * CORES + (i + 1) % CORES) for i in range(reps)]

    def tie(values):
        return lax.optimization_barrier(values)

    def right(value, hop):
        return lax.ppermute(value, "tp", [(i, i + 1) for i in range(hop - 1, ranks - 1)])

    def left(value, hop):
        return lax.ppermute(value, "tp", [(i, i - 1) for i in range(1, ranks - hop + 1)])

    rights, lefts = [tokens], [tokens]
    cuts = [0, slots * 3 // 8, slots * 11 // 16, slots]
    pieces = len(cuts) - 1

    def across(store):
        return lax.ppermute(store, "rep", ring)

    def turn(store):
        return lax.ppermute(store, "rep", swap)

    homes = block_home[replica_variant[rep]]
    holder = homes // slots
    away = (rep // CORES - holder // CORES + chips) % chips
    turned = (rep % CORES + holder % CORES) % CORES
    row_of = (turned * chips + away) * slots + homes % slots
    here = row_of[None, :] == jnp.arange(reps * slots, dtype=jnp.int32)[:, None]
    block_of = jnp.max(jnp.where(here, jnp.arange(blocks, dtype=jnp.int32)[None, :], -1), axis=1)

    deltas = pl.pallas_call(
        functools.partial(scale_kernel, block),
        out_shape=[
            jax.ShapeDtypeStruct(((high - low) * block, width), jnp.bfloat16)
            for low, high in zip(cuts[:-1], cuts[1:])
        ],
        in_specs=[SMEM, VMEM],
        out_specs=[VMEM] * pieces,
        compiler_params=pltpu.CompilerParams(vmem_limit_bytes=VMEM_LIMIT),
        cost_estimate=BRIEF,
    )(delta_scales.astype(jnp.float32), delta_codes)
    held, twins = [deltas], [[turn(delta) for delta in deltas]]
    sent = [across(delta) for delta in deltas]
    turns = [(ranks - 2) * hop // (chips - 1) for hop in range(1, chips)]
    for hop in range(1, ranks):
        came_right, came_left = right(rights[-1], hop), left(lefts[-1], hop)
        if hop == ranks - 1:
            break
        came_right, came_left = tie((came_right, came_left))
        if hop == 1:
            twins[0], came_right, came_left = tie((twins[0], came_right, came_left))
        if hop in turns:
            taken = pieces if len(held) < chips - 1 else 1
            came, rights, lefts = tie((sent[:taken], rights, lefts))
            held.append(came)
            twins.append([turn(value) for value in came])
            sent = [across(value) for value in came] if taken == pieces else sent[taken:]
        rights.append(came_right)
        lefts.append(came_left)

    def merge(weight, chosen):
        parts, stores = [], []
        for core, kept in enumerate((held, twins)):
            for hop, piece in chosen:
                place = (core * chips + hop) * slots
                parts.append((place + cuts[piece], place + cuts[piece + 1]))
                stores.append(kept[hop][piece])
        inputs = [block_of, base_weight] + stores
        given = [] if weight is None else [weight]
        return pl.pallas_call(
            functools.partial(merge_kernel, block, tuple(parts)),
            out_shape=jax.ShapeDtypeStruct((depth, width), jnp.bfloat16),
            in_specs=[SMEM] + [HBM] * (1 + len(stores) + len(given)),
            out_specs=HBM,
            scratch_shapes=[
                pltpu.VMEM((depth, width), jnp.bfloat16),
                pltpu.VMEM((depth, width), jnp.bfloat16),
                pltpu.SemaphoreType.DMA((blocks,)),
                pltpu.SemaphoreType.DMA((blocks,)),
                pltpu.SemaphoreType.DMA((blocks,)),
            ],
            input_output_aliases={len(inputs): 0} if given else {},
            compiler_params=pltpu.CompilerParams(vmem_limit_bytes=VMEM_LIMIT),
            cost_estimate=BRIEF,
        )(*inputs, *given)

    weight = merge(None, [(hop, piece) for hop in range(chips) for piece in range(len(held[hop]))])
    sent, weight = tie((sent, weight))
    held[-1] = held[-1] + sent
    twins[-1] = twins[-1] + [turn(value) for value in sent]
    weight = merge(weight, [(chips - 1, piece) for piece in range(1, pieces)])
    chunks = blocks // CHUNK_BLOCKS

    def product(which, arrays, prior=None):
        last = which == LAST
        count = {ALL: ranks, EARLY: ranks - 1, LAST: 1}[which]
        inputs = [weight] + arrays + ([prior] if last else [])
        scratch = [
            pltpu.VMEM((count * rows, depth), jnp.bfloat16),
            pltpu.VMEM((depth, width), jnp.bfloat16),
            pltpu.VMEM((count * rows, width), jnp.float32),
            pltpu.SemaphoreType.DMA((chunks, ranks + 1)),
        ]
        return pl.pallas_call(
            functools.partial(product_kernel, (ranks, CHUNK_BLOCKS * block, which)),
            out_shape=jax.ShapeDtypeStruct((ranks * rows, width), jnp.bfloat16),
            in_specs=[HBM] * len(inputs),
            out_specs=HBM if last else VMEM,
            scratch_shapes=scratch + ([pltpu.VMEM((rows, width), jnp.bfloat16)] if last else []),
            input_output_aliases={len(inputs) - 1: 0} if last else {},
            compiler_params=pltpu.CompilerParams(vmem_limit_bytes=VMEM_LIMIT),
            cost_estimate=BRIEF,
        )(*inputs)

    (came_right, came_left), weight = tie(((came_right, came_left), weight))
    return product(ALL, rights + [came_right] + lefts[1:] + [came_left])


def solution(mesh):
    in_specs = (
        P(("groups", "rep", "tp"), None),
        P(None, "tp"),
        P(("groups", "rep"), "tp"),
        P(("groups", "rep"), "tp"),
        P("groups"),
        P("groups", None),
    )
    out_specs = P(("groups", "rep"), "tp")
    return jax.shard_map(local, mesh=mesh, in_specs=in_specs, out_specs=out_specs, check_vma=False)
```

```python
import functools
import jax
import jax.numpy as jnp
from jax import lax
from jax.experimental import pallas as pl
from jax.experimental.pallas import tpu as pltpu
from jax.sharding import PartitionSpec as P

CORES = 2
CHUNK_BLOCKS = 8


VMEM_LIMIT = 60 * 1024 * 1024
SMEM = pl.BlockSpec(memory_space=pltpu.SMEM)
VMEM = pl.BlockSpec(memory_space=pltpu.VMEM)
HBM = pl.BlockSpec(memory_space=pl.ANY)
BRIEF = pl.CostEstimate(flops=1, bytes_accessed=1, transcendentals=0)


def scale_kernel(block, scale_ref, codes_ref, *out_refs):
    col_blocks = scale_ref.shape[1]
    wide = codes_ref.shape[1] // col_blocks
    first = 0
    for out_ref in out_refs:
        count = out_ref.shape[0] // block

        @pl.loop(0, count)
        def _(index):
            source = pl.ds(pl.multiple_of((first + index) * block, block), block)
            target = pl.ds(pl.multiple_of(index * block, block), block)
            for col in range(col_blocks):
                at = pl.ds(col * wide, wide)
                delta = codes_ref[source, at].astype(jnp.float32) * scale_ref[first + index, col]
                out_ref[target, at] = delta.astype(jnp.bfloat16)

        first += count


def merge_kernel(block, parts, block_ref, base_ref, *refs):
    stores = refs[: len(parts)]
    out_ref, base_buf, delta_buf, base_sems, delta_sems, out_sems = refs[-6:]

    def rows(index):
        return pl.ds(pl.multiple_of(index * block, block), block)

    def copies(index, store, slot):
        return (
            pltpu.make_async_copy(base_ref.at[rows(index), :], base_buf.at[rows(index), :], base_sems.at[index]),
            pltpu.make_async_copy(store.at[rows(slot), :], delta_buf.at[rows(index), :], delta_sems.at[index]),
        )

    def result(index):
        return pltpu.make_async_copy(base_buf.at[rows(index), :], out_ref.at[rows(index), :], out_sems.at[index])

    def each(visit):
        for (low, high), store in zip(parts, stores):

            @pl.loop(low, high)
            def _(row):
                index = block_ref[row]

                @pl.when(index >= 0)
                def _():
                    visit(index, store, row - low)

    def fetch(index, store, slot):
        for copy in copies(index, store, slot):
            copy.start()

    def merge(index, store, slot):
        for copy in copies(index, store, slot):
            copy.wait()
        merged = base_buf[rows(index), :].astype(jnp.float32) + delta_buf[rows(index), :].astype(jnp.float32)
        base_buf[rows(index), :] = merged.astype(jnp.bfloat16)
        result(index).start()

    each(fetch)
    each(merge)
    each(lambda index, store, slot: result(index).wait())


def product_kernel(dims, weight_ref, *refs):
    ranks, span, last = dims
    given = 2 * ranks - 1 if last else 2 * ranks - 3
    own, rights = refs[0], refs[1 : (given + 1) // 2]
    lefts = refs[(given + 1) // 2 : given]
    out_ref, token_buf, weight_buf, total, sems = refs[-5:] if not last else refs[-6:-1]
    rows, depth = own.shape
    chunks = depth // span
    rank = lax.axis_index("tp")
    star = lax.rem(2 * rank + 1, ranks)

    def columns(chunk):
        return pl.ds(pl.multiple_of(chunk * span, span), span)

    def origin_rows(hop):
        return pl.ds(pl.multiple_of(lax.rem(rank - hop + ranks, ranks) * rows, rows), rows)

    def slot_rows(hop):
        slot = 0 if last else hop - (star < hop).astype(jnp.int32)
        return pl.ds(pl.multiple_of(slot * rows, rows), rows)

    def weight_copy(chunk):
        at = columns(chunk)
        return pltpu.make_async_copy(weight_ref.at[at, :], weight_buf.at[at, :], sems.at[chunk, ranks])

    def token_copy(chunk, hop, source):
        at = columns(chunk)
        return pltpu.make_async_copy(source.at[:, at], token_buf.at[slot_rows(hop), at], sems.at[chunk, hop])

    def each(visit):
        for hop in range(ranks):

            @pl.when((star == hop) if last else (star != hop))
            def _():
                visit(hop)

    def fetch(chunk, hop):
        if hop == 0:
            token_copy(chunk, hop, own).start()
            return
        if hop <= len(rights):

            @pl.when(rank >= hop)
            def _():
                token_copy(chunk, hop, rights[hop - 1]).start()

        if ranks - hop <= len(lefts):

            @pl.when(rank < hop)
            def _():
                token_copy(chunk, hop, lefts[ranks - hop - 1]).start()

    @pl.loop(0, chunks)
    def _(chunk):
        weight_copy(chunk).start()
        each(functools.partial(fetch, chunk))

    total[...] = jnp.zeros_like(total)

    @pl.loop(0, chunks)
    def _(chunk):
        weight_copy(chunk).wait()
        each(lambda hop: token_copy(chunk, hop, own).wait())
        at = columns(chunk)
        total[...] += jnp.dot(token_buf[:, at], weight_buf[at, :], preferred_element_type=jnp.float32)

    if last:
        result = refs[-1]
        result[...] = total[...].astype(result.dtype)

        def store(hop):
            pltpu.sync_copy(result, out_ref.at[origin_rows(hop), :])

    else:

        def store(hop):
            out_ref[origin_rows(hop), :] = total[slot_rows(hop), :].astype(out_ref.dtype)

    each(store)


def local(tokens, base_weight, delta_codes, delta_scales, replica_variant, block_home):
    ranks, reps = lax.axis_size("tp"), lax.axis_size("rep")
    blocks = block_home.shape[1]
    depth, width = base_weight.shape
    rows = tokens.shape[0]
    block = depth // blocks
    slots = delta_scales.shape[0]
    rep = lax.axis_index("rep")
    chips = reps // CORES
    ring = [(i, (i + CORES) % reps) for i in range(reps)]
    swap = [(i, i // CORES * CORES + (i + 1) % CORES) for i in range(reps)]

    def tie(values):
        return lax.optimization_barrier(values)

    def right(value, hop):
        return lax.ppermute(value, "tp", [(i, i + 1) for i in range(hop - 1, ranks - 1)])

    def left(value, hop):
        return lax.ppermute(value, "tp", [(i, i - 1) for i in range(1, ranks - hop + 1)])

    rights, lefts = [tokens], [tokens]
    cuts = [0, slots * 3 // 4, slots]
    pieces = len(cuts) - 1

    def across(store):
        return lax.ppermute(store, "rep", ring)

    def turn(store):
        return lax.ppermute(store, "rep", swap)

    homes = block_home[replica_variant[rep]]
    holder = homes // slots
    away = (rep // CORES - holder // CORES + chips) % chips
    turned = (rep % CORES + holder % CORES) % CORES
    row_of = (turned * chips + away) * slots + homes % slots
    here = row_of[None, :] == jnp.arange(reps * slots, dtype=jnp.int32)[:, None]
    block_of = jnp.max(jnp.where(here, jnp.arange(blocks, dtype=jnp.int32)[None, :], -1), axis=1)

    deltas = pl.pallas_call(
        functools.partial(scale_kernel, block),
        out_shape=[
            jax.ShapeDtypeStruct(((high - low) * block, width), jnp.bfloat16)
            for low, high in zip(cuts[:-1], cuts[1:])
        ],
        in_specs=[SMEM, VMEM],
        out_specs=[VMEM] * pieces,
        compiler_params=pltpu.CompilerParams(vmem_limit_bytes=VMEM_LIMIT),
        cost_estimate=BRIEF,
    )(delta_scales.astype(jnp.float32), delta_codes)
    held, twins = [deltas], [[turn(delta) for delta in deltas]]
    sent = [across(delta) for delta in deltas]
    turns = [(ranks - 2) * hop // (chips - 1) for hop in range(1, chips)]
    for hop in range(1, ranks):
        came_right, came_left = right(rights[-1], hop), left(lefts[-1], hop)
        if hop == ranks - 1:
            break
        rights.append(came_right)
        lefts.append(came_left)
        if hop in turns:
            taken = pieces if len(held) < chips - 1 else 1
            came, twins, tied_right, tied_left = tie((sent[:taken], twins, came_right, came_left))
            kept = [tied_right, tied_left]
            held.append(came)
            twins.append([turn(value) for value in came])
            sent = [across(value) for value in came] if taken == pieces else sent[taken:]

    def merge(weight, chosen):
        parts, stores = [], []
        for core, kept in enumerate((held, twins)):
            for hop, piece in chosen:
                place = (core * chips + hop) * slots
                parts.append((place + cuts[piece], place + cuts[piece + 1]))
                stores.append(kept[hop][piece])
        inputs = [block_of, base_weight] + stores
        given = [] if weight is None else [weight]
        return pl.pallas_call(
            functools.partial(merge_kernel, block, tuple(parts)),
            out_shape=jax.ShapeDtypeStruct((depth, width), jnp.bfloat16),
            in_specs=[SMEM] + [HBM] * (1 + len(stores) + len(given)),
            out_specs=HBM,
            scratch_shapes=[
                pltpu.VMEM((depth, width), jnp.bfloat16),
                pltpu.VMEM((depth, width), jnp.bfloat16),
                pltpu.SemaphoreType.DMA((blocks,)),
                pltpu.SemaphoreType.DMA((blocks,)),
                pltpu.SemaphoreType.DMA((blocks,)),
            ],
            input_output_aliases={len(inputs): 0} if given else {},
            compiler_params=pltpu.CompilerParams(vmem_limit_bytes=VMEM_LIMIT),
            cost_estimate=BRIEF,
        )(*inputs, *given)

    there = [(hop, piece) for hop, values in enumerate(held) for piece in range(len(values))]
    weight = merge(None, there)
    sent, weight = tie((sent, weight))
    held[-1] = held[-1] + sent
    twins[-1] = twins[-1] + [turn(value) for value in sent]
    weight = merge(weight, [(chips - 1, piece) for piece in range(1, pieces)])
    chunks = blocks // CHUNK_BLOCKS

    def product(arrays, prior):
        last = prior is not None
        count = 1 if last else ranks - 1
        inputs = [weight] + arrays + ([prior] if last else [])
        scratch = [
            pltpu.VMEM((count * rows, depth), jnp.bfloat16),
            pltpu.VMEM((depth, width), jnp.bfloat16),
            pltpu.VMEM((count * rows, width), jnp.float32),
            pltpu.SemaphoreType.DMA((chunks, ranks + 1)),
        ]
        return pl.pallas_call(
            functools.partial(product_kernel, (ranks, CHUNK_BLOCKS * block, last)),
            out_shape=jax.ShapeDtypeStruct((ranks * rows, width), jnp.bfloat16),
            in_specs=[HBM] * len(inputs),
            out_specs=HBM if last else VMEM,
            scratch_shapes=scratch + ([pltpu.VMEM((rows, width), jnp.bfloat16)] if last else []),
            input_output_aliases={len(inputs) - 1: 0} if last else {},
            compiler_params=pltpu.CompilerParams(vmem_limit_bytes=VMEM_LIMIT),
            cost_estimate=BRIEF,
        )(*inputs)

    early = product(rights[:-1] + kept[:1] + lefts[1:-1] + kept[1:], None)
    (came_right, came_left), early = tie(((came_right, came_left), early))
    return product(rights + [came_right] + lefts[1:] + [came_left], early)


def solution(mesh):
    in_specs = (
        P(("groups", "rep", "tp"), None),
        P(None, "tp"),
        P(("groups", "rep"), "tp"),
        P(("groups", "rep"), "tp"),
        P("groups"),
        P("groups", None),
    )
    out_specs = P(("groups", "rep"), "tp")
    return jax.shard_map(local, mesh=mesh, in_specs=in_specs, out_specs=out_specs, check_vma=False)
```

```python
import functools
import jax
import jax.numpy as jnp
from jax import lax
from jax.experimental import pallas as pl
from jax.experimental.pallas import tpu as pltpu
from jax.sharding import PartitionSpec as P

CORES = 2
CHUNK_BLOCKS = 8


VMEM_LIMIT = 60 * 1024 * 1024
SMEM = pl.BlockSpec(memory_space=pltpu.SMEM)
VMEM = pl.BlockSpec(memory_space=pltpu.VMEM)
HBM = pl.BlockSpec(memory_space=pl.ANY)
BRIEF = pl.CostEstimate(flops=1, bytes_accessed=1, transcendentals=0)


def scale_kernel(block, scale_ref, codes_ref, *out_refs):
    col_blocks = scale_ref.shape[1]
    wide = codes_ref.shape[1] // col_blocks
    first = 0
    for out_ref in out_refs:
        count = out_ref.shape[0] // block

        @pl.loop(0, count)
        def _(index):
            source = pl.ds(pl.multiple_of((first + index) * block, block), block)
            target = pl.ds(pl.multiple_of(index * block, block), block)
            for col in range(col_blocks):
                at = pl.ds(col * wide, wide)
                delta = codes_ref[source, at].astype(jnp.float32) * scale_ref[first + index, col]
                out_ref[target, at] = delta.astype(jnp.bfloat16)

        first += count


def merge_kernel(block, parts, block_ref, base_ref, *refs):
    stores = refs[: len(parts)]
    out_ref, base_buf, delta_buf, base_sems, delta_sems, out_sems = refs[-6:]

    def rows(index):
        return pl.ds(pl.multiple_of(index * block, block), block)

    def copies(index, store, slot):
        return (
            pltpu.make_async_copy(base_ref.at[rows(index), :], base_buf.at[rows(index), :], base_sems.at[index]),
            pltpu.make_async_copy(store.at[rows(slot), :], delta_buf.at[rows(index), :], delta_sems.at[index]),
        )

    def result(index):
        return pltpu.make_async_copy(base_buf.at[rows(index), :], out_ref.at[rows(index), :], out_sems.at[index])

    def each(visit):
        for (low, high), store in zip(parts, stores):

            @pl.loop(low, high)
            def _(row):
                index = block_ref[row]

                @pl.when(index >= 0)
                def _():
                    visit(index, store, row - low)

    def fetch(index, store, slot):
        for copy in copies(index, store, slot):
            copy.start()

    def merge(index, store, slot):
        for copy in copies(index, store, slot):
            copy.wait()
        merged = base_buf[rows(index), :].astype(jnp.float32) + delta_buf[rows(index), :].astype(jnp.float32)
        base_buf[rows(index), :] = merged.astype(jnp.bfloat16)
        result(index).start()

    each(fetch)
    each(merge)
    each(lambda index, store, slot: result(index).wait())


def product_kernel(dims, weight_ref, *refs):
    ranks, span, last = dims
    given = 2 * ranks - 1 if last else 2 * ranks - 3
    own, rights = refs[0], refs[1 : (given + 1) // 2]
    lefts = refs[(given + 1) // 2 : given]
    out_ref, token_buf, total, sems = refs[-5:-1] if last else refs[-4:]
    result = refs[-1]
    rows, depth = own.shape
    chunks = depth // span
    rank = lax.axis_index("tp")
    star = lax.rem(2 * rank + 1, ranks)

    def columns(chunk):
        return pl.ds(pl.multiple_of(chunk * span, span), span)

    def origin_rows(hop):
        return pl.ds(pl.multiple_of(lax.rem(rank - hop + ranks, ranks) * rows, rows), rows)

    def slot_rows(hop):
        slot = 0 if last else hop - (star < hop).astype(jnp.int32)
        return pl.ds(pl.multiple_of(slot * rows, rows), rows)

    def token_copy(chunk, hop, source):
        at = columns(chunk)
        return pltpu.make_async_copy(source.at[:, at], token_buf.at[slot_rows(hop), at], sems.at[chunk, hop])

    def each(visit):
        for hop in range(ranks):

            @pl.when((star == hop) if last else (star != hop))
            def _():
                visit(hop)

    def fetch(chunk, hop):
        if hop == 0:
            token_copy(chunk, hop, own).start()
            return
        if hop <= len(rights):

            @pl.when(rank >= hop)
            def _():
                token_copy(chunk, hop, rights[hop - 1]).start()

        if ranks - hop <= len(lefts):

            @pl.when(rank < hop)
            def _():
                token_copy(chunk, hop, lefts[ranks - hop - 1]).start()

    @pl.loop(0, chunks)
    def _(chunk):
        each(functools.partial(fetch, chunk))

    total[...] = jnp.zeros_like(total)

    @pl.loop(0, chunks)
    def _(chunk):
        each(lambda hop: token_copy(chunk, hop, own).wait())
        at = columns(chunk)
        total[...] += jnp.dot(token_buf[:, at], weight_ref[at, :], preferred_element_type=jnp.float32)

    if last:
        result[...] = total[...].astype(result.dtype)

        def store(hop):
            pltpu.sync_copy(result, out_ref.at[origin_rows(hop), :])

    else:

        def store(hop):
            out_ref[origin_rows(hop), :] = total[slot_rows(hop), :].astype(out_ref.dtype)

    each(store)


def local(tokens, base_weight, delta_codes, delta_scales, replica_variant, block_home):
    ranks, reps = lax.axis_size("tp"), lax.axis_size("rep")
    blocks = block_home.shape[1]
    depth, width = base_weight.shape
    rows = tokens.shape[0]
    block = depth // blocks
    slots = delta_scales.shape[0]
    rep = lax.axis_index("rep")
    chips = reps // CORES
    ring = [(i, (i + CORES) % reps) for i in range(reps)]
    swap = [(i, i // CORES * CORES + (i + 1) % CORES) for i in range(reps)]

    def tie(values):
        return lax.optimization_barrier(values)

    def right(value, hop):
        return lax.ppermute(value, "tp", [(i, i + 1) for i in range(hop - 1, ranks - 1)])

    def left(value, hop):
        return lax.ppermute(value, "tp", [(i, i - 1) for i in range(1, ranks - hop + 1)])

    rights, lefts = [tokens], [tokens]
    cuts = [0, slots * 3 // 4, slots]
    pieces = len(cuts) - 1

    def across(store):
        return lax.ppermute(store, "rep", ring)

    def turn(store):
        return lax.ppermute(store, "rep", swap)

    homes = block_home[replica_variant[rep]]
    holder = homes // slots
    away = (rep // CORES - holder // CORES + chips) % chips
    turned = (rep % CORES + holder % CORES) % CORES
    row_of = (turned * chips + away) * slots + homes % slots
    here = row_of[None, :] == jnp.arange(reps * slots, dtype=jnp.int32)[:, None]
    block_of = jnp.max(jnp.where(here, jnp.arange(blocks, dtype=jnp.int32)[None, :], -1), axis=1)

    deltas = pl.pallas_call(
        functools.partial(scale_kernel, block),
        out_shape=[
            jax.ShapeDtypeStruct(((high - low) * block, width), jnp.bfloat16)
            for low, high in zip(cuts[:-1], cuts[1:])
        ],
        in_specs=[SMEM, VMEM],
        out_specs=[VMEM] * pieces,
        compiler_params=pltpu.CompilerParams(vmem_limit_bytes=VMEM_LIMIT),
        cost_estimate=BRIEF,
    )(delta_scales.astype(jnp.float32), delta_codes)
    held, twins = [deltas], [[turn(delta) for delta in deltas]]
    sent = [across(delta) for delta in deltas]
    turns = [(ranks - 2) * hop // (chips - 1) for hop in range(1, chips)]
    for hop in range(1, ranks):
        came_right, came_left = right(rights[-1], hop), left(lefts[-1], hop)
        if hop == ranks - 1:
            break
        rights.append(came_right)
        lefts.append(came_left)
        if hop in turns:
            taken = pieces if len(held) < chips - 1 else 1
            came, twins, tied_right, tied_left = tie((sent[:taken], twins, came_right, came_left))
            kept = [tied_right, tied_left]
            held.append(came)
            twins.append([turn(value) for value in came])
            sent = [across(value) for value in came] if taken == pieces else sent[taken:]

    def merge(weight, chosen):
        parts, stores = [], []
        for core, kept in enumerate((held, twins)):
            for hop, piece in chosen:
                place = (core * chips + hop) * slots
                parts.append((place + cuts[piece], place + cuts[piece + 1]))
                stores.append(kept[hop][piece])
        inputs = [block_of, base_weight] + stores
        given = [] if weight is None else [weight]
        return pl.pallas_call(
            functools.partial(merge_kernel, block, tuple(parts)),
            out_shape=jax.ShapeDtypeStruct((depth, width), jnp.bfloat16),
            in_specs=[SMEM] + [HBM] * (1 + len(stores) + len(given)),
            out_specs=HBM,
            scratch_shapes=[
                pltpu.VMEM((depth, width), jnp.bfloat16),
                pltpu.VMEM((depth, width), jnp.bfloat16),
                pltpu.SemaphoreType.DMA((blocks,)),
                pltpu.SemaphoreType.DMA((blocks,)),
                pltpu.SemaphoreType.DMA((blocks,)),
            ],
            input_output_aliases={len(inputs): 0} if given else {},
            compiler_params=pltpu.CompilerParams(vmem_limit_bytes=VMEM_LIMIT),
            cost_estimate=BRIEF,
        )(*inputs, *given)

    there = [(hop, piece) for hop, values in enumerate(held) for piece in range(len(values))]
    weight = merge(None, there)
    sent, weight = tie((sent, weight))
    held[-1] = held[-1] + sent
    twins[-1] = twins[-1] + [turn(value) for value in sent]
    weight = merge(weight, [(chips - 1, piece) for piece in range(1, pieces)])
    chunks = blocks // CHUNK_BLOCKS

    def product(arrays, prior):
        last = prior is not None
        count = 1 if last else ranks - 1
        inputs = [weight] + arrays + ([prior] if last else [])
        need = 2 * (count * rows + width) * depth + 12 * count * rows * width + 6 * 1024 * 1024
        buffers = [pltpu.VMEM((count * rows, depth), jnp.bfloat16)]
        buffers += [pltpu.VMEM((count * rows, width), jnp.float32), pltpu.SemaphoreType.DMA((chunks, ranks + 1))]
        buffers += [pltpu.VMEM((rows, width), jnp.bfloat16)] if last else []
        return pl.pallas_call(
            functools.partial(product_kernel, (ranks, CHUNK_BLOCKS * block, last)),
            out_shape=jax.ShapeDtypeStruct((ranks * rows, width), jnp.bfloat16),
            in_specs=[VMEM] + [HBM] * (len(inputs) - 1),
            out_specs=HBM if last else VMEM,
            scratch_shapes=buffers,
            input_output_aliases={len(inputs) - 1: 0} if last else {},
            compiler_params=pltpu.CompilerParams(vmem_limit_bytes=need),
            cost_estimate=BRIEF,
        )(*inputs)

    early = product(rights[:-1] + kept[:1] + lefts[1:-1] + kept[1:], None)
    (came_right, came_left), early = tie(((came_right, came_left), early))
    return product(rights + [came_right] + lefts[1:] + [came_left], early)


def solution(mesh):
    in_specs = (
        P(("groups", "rep", "tp"), None),
        P(None, "tp"),
        P(("groups", "rep"), "tp"),
        P(("groups", "rep"), "tp"),
        P("groups"),
        P("groups", None),
    )
    out_specs = P(("groups", "rep"), "tp")
    return jax.shard_map(local, mesh=mesh, in_specs=in_specs, out_specs=out_specs, check_vma=False)
```

```python
import functools
import jax
import jax.numpy as jnp
from jax import lax
from jax.experimental import pallas as pl
from jax.experimental.pallas import tpu as pltpu
from jax.sharding import PartitionSpec as P

CORES = 2
CHUNK_BLOCKS = 8


VMEM_LIMIT = 60 * 1024 * 1024
SMEM = pl.BlockSpec(memory_space=pltpu.SMEM)
VMEM = pl.BlockSpec(memory_space=pltpu.VMEM)
HBM = pl.BlockSpec(memory_space=pl.ANY)
BRIEF = pl.CostEstimate(flops=1, bytes_accessed=1, transcendentals=0)


def scale_kernel(block, scale_ref, codes_ref, *out_refs):
    scales = scale_ref[...].astype(jnp.float32)
    col_blocks = scales.shape[0]
    wide = codes_ref.shape[1] // col_blocks
    first = 0
    for out_ref in out_refs:
        count = out_ref.shape[0] // block
        for index in range(count):
            slot = first + index
            for col in range(col_blocks):
                at = pl.ds(col * wide, wide)
                delta = codes_ref[pl.ds(slot * block, block), at].astype(jnp.float32)
                delta = delta * scales[col : col + 1, slot : slot + 1]
                out_ref[pl.ds(index * block, block), at] = delta.astype(jnp.bfloat16)
        first += count


def merge_kernel(block, parts, block_ref, base_ref, *refs):
    stores = refs[: len(parts)]
    out_ref, base_buf, delta_buf, base_sems, delta_sems, out_sems = refs[-6:]

    def rows(index):
        return pl.ds(pl.multiple_of(index * block, block), block)

    def copies(index, store, slot):
        return (
            pltpu.make_async_copy(base_ref.at[rows(index), :], base_buf.at[rows(index), :], base_sems.at[index]),
            pltpu.make_async_copy(store.at[rows(slot), :], delta_buf.at[rows(index), :], delta_sems.at[index]),
        )

    def result(index):
        return pltpu.make_async_copy(base_buf.at[rows(index), :], out_ref.at[rows(index), :], out_sems.at[index])

    def each(visit):
        for (low, high), store in zip(parts, stores):

            @pl.loop(low, high)
            def _(row):
                index = block_ref[row]

                @pl.when(index >= 0)
                def _():
                    visit(index, store, row - low)

    def fetch(index, store, slot):
        for copy in copies(index, store, slot):
            copy.start()

    def merge(index, store, slot):
        for copy in copies(index, store, slot):
            copy.wait()
        merged = base_buf[rows(index), :].astype(jnp.float32) + delta_buf[rows(index), :].astype(jnp.float32)
        base_buf[rows(index), :] = merged.astype(jnp.bfloat16)
        result(index).start()

    each(fetch)
    each(merge)
    each(lambda index, store, slot: result(index).wait())


def product_kernel(dims, weight_ref, *refs):
    ranks, span, last = dims
    given = 2 * ranks - 1 if last else 2 * ranks - 3
    own, rights = refs[0], refs[1 : (given + 1) // 2]
    lefts = refs[(given + 1) // 2 : given]
    out_ref, token_buf, weight_buf, total, sems = refs[-5:] if not last else refs[-6:-1]
    rows, depth = own.shape
    chunks = depth // span
    rank = lax.axis_index("tp")
    star = lax.rem(2 * rank + 1, ranks)

    def columns(chunk):
        return pl.ds(pl.multiple_of(chunk * span, span), span)

    def origin_rows(hop):
        return pl.ds(pl.multiple_of(lax.rem(rank - hop + ranks, ranks) * rows, rows), rows)

    def slot_rows(hop):
        slot = 0 if last else hop - (star < hop).astype(jnp.int32)
        return pl.ds(pl.multiple_of(slot * rows, rows), rows)

    def weight_copy(chunk):
        at = columns(chunk)
        return pltpu.make_async_copy(weight_ref.at[at, :], weight_buf.at[at, :], sems.at[chunk, ranks])

    def token_copy(chunk, hop, source):
        at = columns(chunk)
        return pltpu.make_async_copy(source.at[:, at], token_buf.at[slot_rows(hop), at], sems.at[chunk, hop])

    def each(visit):
        for hop in range(ranks):

            @pl.when((star == hop) if last else (star != hop))
            def _():
                visit(hop)

    def fetch(chunk, hop):
        if hop == 0:
            token_copy(chunk, hop, own).start()
            return
        if hop <= len(rights):

            @pl.when(rank >= hop)
            def _():
                token_copy(chunk, hop, rights[hop - 1]).start()

        if ranks - hop <= len(lefts):

            @pl.when(rank < hop)
            def _():
                token_copy(chunk, hop, lefts[ranks - hop - 1]).start()

    @pl.loop(0, chunks)
    def _(chunk):
        weight_copy(chunk).start()
        each(functools.partial(fetch, chunk))

    total[...] = jnp.zeros_like(total)

    @pl.loop(0, chunks)
    def _(chunk):
        weight_copy(chunk).wait()
        each(lambda hop: token_copy(chunk, hop, own).wait())
        at = columns(chunk)
        total[...] += jnp.dot(token_buf[:, at], weight_buf[at, :], preferred_element_type=jnp.float32)

    if last:
        result = refs[-1]
        result[...] = total[...].astype(result.dtype)

        def store(hop):
            pltpu.sync_copy(result, out_ref.at[origin_rows(hop), :])

    else:

        def store(hop):
            out_ref[origin_rows(hop), :] = total[slot_rows(hop), :].astype(out_ref.dtype)

    each(store)


def local(tokens, base_weight, delta_codes, delta_scales, replica_variant, block_home):
    ranks, reps = lax.axis_size("tp"), lax.axis_size("rep")
    blocks = block_home.shape[1]
    depth, width = base_weight.shape
    rows = tokens.shape[0]
    block = depth // blocks
    slots = delta_scales.shape[0]
    rep = lax.axis_index("rep")
    chips = reps // CORES
    ring = [(i, (i + CORES) % reps) for i in range(reps)]
    swap = [(i, i // CORES * CORES + (i + 1) % CORES) for i in range(reps)]

    def tie(values):
        return lax.optimization_barrier(values)

    def right(value, hop):
        return lax.ppermute(value, "tp", [(i, i + 1) for i in range(hop - 1, ranks - 1)])

    def left(value, hop):
        return lax.ppermute(value, "tp", [(i, i - 1) for i in range(1, ranks - hop + 1)])

    rights, lefts = [tokens], [tokens]
    cuts = [0, slots * 3 // 4, slots]
    pieces = len(cuts) - 1

    def across(store):
        return lax.ppermute(store, "rep", ring)

    def turn(store):
        return lax.ppermute(store, "rep", swap)

    homes = block_home[replica_variant[rep]]
    holder = homes // slots
    away = (rep // CORES - holder // CORES + chips) % chips
    turned = (rep % CORES + holder % CORES) % CORES
    row_of = (turned * chips + away) * slots + homes % slots
    here = row_of[None, :] == jnp.arange(reps * slots, dtype=jnp.int32)[:, None]
    block_of = jnp.max(jnp.where(here, jnp.arange(blocks, dtype=jnp.int32)[None, :], -1), axis=1)

    deltas = pl.pallas_call(
        functools.partial(scale_kernel, block),
        out_shape=[
            jax.ShapeDtypeStruct(((high - low) * block, width), jnp.bfloat16)
            for low, high in zip(cuts[:-1], cuts[1:])
        ],
        in_specs=[VMEM, VMEM],
        out_specs=[VMEM] * pieces,
        compiler_params=pltpu.CompilerParams(vmem_limit_bytes=VMEM_LIMIT),
        cost_estimate=BRIEF,
    )(delta_scales.T, delta_codes)
    held, twins = [deltas], [[turn(delta) for delta in deltas]]
    sent = [across(delta) for delta in deltas]
    turns = [(ranks - 2) * hop // (chips - 1) for hop in range(1, chips)]
    for hop in range(1, ranks):
        came_right, came_left = right(rights[-1], hop), left(lefts[-1], hop)
        if hop == ranks - 1:
            break
        rights.append(came_right)
        lefts.append(came_left)
        if hop in turns:
            taken = pieces if len(held) < chips - 1 else 1
            came, twins, tied_right, tied_left = tie((sent[:taken], twins, came_right, came_left))
            kept = [tied_right, tied_left]
            held.append(came)
            twins.append([turn(value) for value in came])
            sent = [across(value) for value in came] if taken == pieces else sent[taken:]

    def merge(weight, chosen):
        parts, stores = [], []
        for core, kept in enumerate((held, twins)):
            for hop, piece in chosen:
                place = (core * chips + hop) * slots
                parts.append((place + cuts[piece], place + cuts[piece + 1]))
                stores.append(kept[hop][piece])
        inputs = [block_of, base_weight] + stores
        given = [] if weight is None else [weight]
        return pl.pallas_call(
            functools.partial(merge_kernel, block, tuple(parts)),
            out_shape=jax.ShapeDtypeStruct((depth, width), jnp.bfloat16),
            in_specs=[SMEM] + [HBM] * (1 + len(stores) + len(given)),
            out_specs=HBM,
            scratch_shapes=[
                pltpu.VMEM((depth, width), jnp.bfloat16),
                pltpu.VMEM((depth, width), jnp.bfloat16),
                pltpu.SemaphoreType.DMA((blocks,)),
                pltpu.SemaphoreType.DMA((blocks,)),
                pltpu.SemaphoreType.DMA((blocks,)),
            ],
            input_output_aliases={len(inputs): 0} if given else {},
            compiler_params=pltpu.CompilerParams(vmem_limit_bytes=VMEM_LIMIT),
            cost_estimate=BRIEF,
        )(*inputs, *given)

    there = [(hop, piece) for hop, values in enumerate(held) for piece in range(len(values))]
    weight = merge(None, there)
    sent, weight = tie((sent, weight))
    held[-1] = held[-1] + sent
    twins[-1] = twins[-1] + [turn(value) for value in sent]
    weight = merge(weight, [(chips - 1, piece) for piece in range(1, pieces)])
    chunks = blocks // CHUNK_BLOCKS

    def product(arrays, prior):
        last = prior is not None
        count = 1 if last else ranks - 1
        inputs = [weight] + arrays + ([prior] if last else [])
        scratch = [
            pltpu.VMEM((count * rows, depth), jnp.bfloat16),
            pltpu.VMEM((depth, width), jnp.bfloat16),
            pltpu.VMEM((count * rows, width), jnp.float32),
            pltpu.SemaphoreType.DMA((chunks, ranks + 1)),
        ]
        return pl.pallas_call(
            functools.partial(product_kernel, (ranks, CHUNK_BLOCKS * block, last)),
            out_shape=jax.ShapeDtypeStruct((ranks * rows, width), jnp.bfloat16),
            in_specs=[HBM] * len(inputs),
            out_specs=HBM if last else VMEM,
            scratch_shapes=scratch + ([pltpu.VMEM((rows, width), jnp.bfloat16)] if last else []),
            input_output_aliases={len(inputs) - 1: 0} if last else {},
            compiler_params=pltpu.CompilerParams(vmem_limit_bytes=VMEM_LIMIT),
            cost_estimate=BRIEF,
        )(*inputs)

    early = product(rights[:-1] + kept[:1] + lefts[1:-1] + kept[1:], None)
    (came_right, came_left), early = tie(((came_right, came_left), early))
    return product(rights + [came_right] + lefts[1:] + [came_left], early)


def solution(mesh):
    in_specs = (
        P(("groups", "rep", "tp"), None),
        P(None, "tp"),
        P(("groups", "rep"), "tp"),
        P(("groups", "rep"), "tp"),
        P("groups"),
        P("groups", None),
    )
    out_specs = P(("groups", "rep"), "tp")
    return jax.shard_map(local, mesh=mesh, in_specs=in_specs, out_specs=out_specs, check_vma=False)
```

```python
import functools
import jax
import jax.numpy as jnp
from jax import lax
from jax.experimental import pallas as pl
from jax.experimental.pallas import tpu as pltpu
from jax.sharding import PartitionSpec as P

CORES = 2
CHUNK_BLOCKS = 8


VMEM_LIMIT = 60 * 1024 * 1024
SMEM = pl.BlockSpec(memory_space=pltpu.SMEM)
VMEM = pl.BlockSpec(memory_space=pltpu.VMEM)
HBM = pl.BlockSpec(memory_space=pl.ANY)
BRIEF = pl.CostEstimate(flops=1, bytes_accessed=1, transcendentals=0)


def scale_kernel(block, scale_ref, codes_ref, *out_refs):
    scales = scale_ref[...].astype(jnp.float32)
    col_blocks = scales.shape[0]
    wide = codes_ref.shape[1] // col_blocks
    first = 0
    for out_ref in out_refs:
        count = out_ref.shape[0] // block
        for index in range(count):
            slot = first + index
            for col in range(col_blocks):
                at = pl.ds(col * wide, wide)
                delta = codes_ref[pl.ds(slot * block, block), at].astype(jnp.float32)
                delta = delta * scales[col : col + 1, slot : slot + 1]
                out_ref[pl.ds(index * block, block), at] = delta.astype(jnp.bfloat16)
        first += count


def merge_kernel(block, parts, block_ref, base_ref, *refs):
    stores = refs[: len(parts)]
    out_ref, base_buf, delta_buf, base_sems, delta_sems, out_sems = refs[-6:]

    def rows(index):
        return pl.ds(pl.multiple_of(index * block, block), block)

    def copies(index, store, slot):
        return (
            pltpu.make_async_copy(base_ref.at[rows(index), :], base_buf.at[rows(index), :], base_sems.at[index]),
            pltpu.make_async_copy(store.at[rows(slot), :], delta_buf.at[rows(index), :], delta_sems.at[index]),
        )

    def result(index):
        return pltpu.make_async_copy(base_buf.at[rows(index), :], out_ref.at[rows(index), :], out_sems.at[index])

    def each(visit):
        for (low, high), store in zip(parts, stores):

            @pl.loop(low, high)
            def _(row):
                index = block_ref[row]

                @pl.when(index >= 0)
                def _():
                    visit(index, store, row - low)

    def fetch(index, store, slot):
        for copy in copies(index, store, slot):
            copy.start()

    def merge(index, store, slot):
        for copy in copies(index, store, slot):
            copy.wait()
        merged = base_buf[rows(index), :].astype(jnp.float32) + delta_buf[rows(index), :].astype(jnp.float32)
        base_buf[rows(index), :] = merged.astype(jnp.bfloat16)
        result(index).start()

    each(fetch)
    each(merge)
    each(lambda index, store, slot: result(index).wait())


def product_kernel(dims, weight_ref, *refs):
    ranks, span, last = dims
    given = 2 * ranks - 1 if last else 2 * ranks - 3
    own, rights = refs[0], refs[1 : (given + 1) // 2]
    lefts = refs[(given + 1) // 2 : given]
    out_ref, token_buf, weight_buf, total, sems = refs[-5:] if not last else refs[-6:-1]
    rows, depth = own.shape
    chunks = depth // span
    rank = lax.axis_index("tp")
    star = lax.rem(2 * rank + 1, ranks)

    def columns(chunk):
        start = chunk * span
        return pl.ds(start if isinstance(start, int) else pl.multiple_of(start, span), span)

    def origin_rows(hop):
        return pl.ds(pl.multiple_of(lax.rem(rank - hop + ranks, ranks) * rows, rows), rows)

    def slot_rows(hop):
        slot = 0 if last else hop - (star < hop).astype(jnp.int32)
        return pl.ds(pl.multiple_of(slot * rows, rows), rows)

    def weight_copy(chunk):
        at = columns(chunk)
        return pltpu.make_async_copy(weight_ref.at[at, :], weight_buf.at[at, :], sems.at[chunk, ranks])

    def token_copy(chunk, hop, source):
        at = columns(chunk)
        return pltpu.make_async_copy(source.at[:, at], token_buf.at[slot_rows(hop), at], sems.at[chunk, hop])

    def each(visit):
        for hop in range(ranks):

            @pl.when((star == hop) if last else (star != hop))
            def _():
                visit(hop)

    def fetch(chunk, hop):
        if hop == 0:
            token_copy(chunk, hop, own).start()
            return
        if hop <= len(rights):

            @pl.when(rank >= hop)
            def _():
                token_copy(chunk, hop, rights[hop - 1]).start()

        if ranks - hop <= len(lefts):

            @pl.when(rank < hop)
            def _():
                token_copy(chunk, hop, lefts[ranks - hop - 1]).start()

    @pl.loop(0, chunks)
    def _(chunk):
        weight_copy(chunk).start()
        each(functools.partial(fetch, chunk))

    total[...] = jnp.zeros_like(total)

    def add(chunk):
        weight_copy(chunk).wait()
        each(lambda hop: token_copy(chunk, hop, own).wait())
        at = columns(chunk)
        total[...] += jnp.dot(token_buf[:, at], weight_buf[at, :], preferred_element_type=jnp.float32)

    if last:
        for chunk in range(chunks):
            add(chunk)
    else:
        pl.loop(0, chunks)(add)

    if last:
        result = refs[-1]
        result[...] = total[...].astype(result.dtype)

        def store(hop):
            pltpu.sync_copy(result, out_ref.at[origin_rows(hop), :])

    else:

        def store(hop):
            out_ref[origin_rows(hop), :] = total[slot_rows(hop), :].astype(out_ref.dtype)

    each(store)


def local(tokens, base_weight, delta_codes, delta_scales, replica_variant, block_home):
    ranks, reps = lax.axis_size("tp"), lax.axis_size("rep")
    blocks = block_home.shape[1]
    depth, width = base_weight.shape
    rows = tokens.shape[0]
    block = depth // blocks
    slots = delta_scales.shape[0]
    rep = lax.axis_index("rep")
    chips = reps // CORES
    ring = [(i, (i + CORES) % reps) for i in range(reps)]
    swap = [(i, i // CORES * CORES + (i + 1) % CORES) for i in range(reps)]

    def tie(values):
        return lax.optimization_barrier(values)

    def right(value, hop):
        return lax.ppermute(value, "tp", [(i, i + 1) for i in range(hop - 1, ranks - 1)])

    def left(value, hop):
        return lax.ppermute(value, "tp", [(i, i - 1) for i in range(1, ranks - hop + 1)])

    rights, lefts = [tokens], [tokens]
    cuts = [0, slots * 3 // 4, slots]
    pieces = len(cuts) - 1

    def across(store):
        return lax.ppermute(store, "rep", ring)

    def turn(store):
        return lax.ppermute(store, "rep", swap)

    homes = block_home[replica_variant[rep]]
    holder = homes // slots
    away = (rep // CORES - holder // CORES + chips) % chips
    turned = (rep % CORES + holder % CORES) % CORES
    row_of = (turned * chips + away) * slots + homes % slots
    here = row_of[None, :] == jnp.arange(reps * slots, dtype=jnp.int32)[:, None]
    block_of = jnp.max(jnp.where(here, jnp.arange(blocks, dtype=jnp.int32)[None, :], -1), axis=1)

    deltas = pl.pallas_call(
        functools.partial(scale_kernel, block),
        out_shape=[
            jax.ShapeDtypeStruct(((high - low) * block, width), jnp.bfloat16)
            for low, high in zip(cuts[:-1], cuts[1:])
        ],
        in_specs=[VMEM, VMEM],
        out_specs=[VMEM] * pieces,
        compiler_params=pltpu.CompilerParams(vmem_limit_bytes=VMEM_LIMIT),
        cost_estimate=BRIEF,
    )(delta_scales.T, delta_codes)
    held, twins = [deltas], [[turn(delta) for delta in deltas]]
    sent = [across(delta) for delta in deltas]
    turns = [(ranks - 2) * hop // (chips - 1) for hop in range(1, chips)]
    for hop in range(1, ranks):
        came_right, came_left = right(rights[-1], hop), left(lefts[-1], hop)
        if hop == ranks - 1:
            break
        rights.append(came_right)
        lefts.append(came_left)
        if hop in turns:
            taken = pieces if len(held) < chips - 1 else 1
            came, twins, tied_right, tied_left = tie((sent[:taken], twins, came_right, came_left))
            kept = [tied_right, tied_left]
            held.append(came)
            twins.append([turn(value) for value in came])
            sent = [across(value) for value in came] if taken == pieces else sent[taken:]

    def merge(weight, chosen):
        parts, stores = [], []
        for core, kept in enumerate((held, twins)):
            for hop, piece in chosen:
                place = (core * chips + hop) * slots
                parts.append((place + cuts[piece], place + cuts[piece + 1]))
                stores.append(kept[hop][piece])
        inputs = [block_of, base_weight] + stores
        given = [] if weight is None else [weight]
        return pl.pallas_call(
            functools.partial(merge_kernel, block, tuple(parts)),
            out_shape=jax.ShapeDtypeStruct((depth, width), jnp.bfloat16),
            in_specs=[SMEM] + [HBM] * (1 + len(stores) + len(given)),
            out_specs=HBM,
            scratch_shapes=[
                pltpu.VMEM((depth, width), jnp.bfloat16),
                pltpu.VMEM((depth, width), jnp.bfloat16),
                pltpu.SemaphoreType.DMA((blocks,)),
                pltpu.SemaphoreType.DMA((blocks,)),
                pltpu.SemaphoreType.DMA((blocks,)),
            ],
            input_output_aliases={len(inputs): 0} if given else {},
            compiler_params=pltpu.CompilerParams(vmem_limit_bytes=VMEM_LIMIT),
            cost_estimate=BRIEF,
        )(*inputs, *given)

    there = [(hop, piece) for hop, values in enumerate(held) for piece in range(len(values))]
    weight = merge(None, there)
    sent, weight = tie((sent, weight))
    held[-1] = held[-1] + sent
    twins[-1] = twins[-1] + [turn(value) for value in sent]
    weight = merge(weight, [(chips - 1, piece) for piece in range(1, pieces)])
    def product(arrays, prior):
        last = prior is not None
        count = 1 if last else ranks - 1
        span = CHUNK_BLOCKS * block * (2 if last else 1)
        inputs = [weight] + arrays + ([prior] if last else [])
        scratch = [
            pltpu.VMEM((count * rows, depth), jnp.bfloat16),
            pltpu.VMEM((depth, width), jnp.bfloat16),
            pltpu.VMEM((count * rows, width), jnp.float32),
            pltpu.SemaphoreType.DMA((depth // span, ranks + 1)),
        ]
        return pl.pallas_call(
            functools.partial(product_kernel, (ranks, span, last)),
            out_shape=jax.ShapeDtypeStruct((ranks * rows, width), jnp.bfloat16),
            in_specs=[HBM] * len(inputs),
            out_specs=HBM if last else VMEM,
            scratch_shapes=scratch + ([pltpu.VMEM((rows, width), jnp.bfloat16)] if last else []),
            input_output_aliases={len(inputs) - 1: 0} if last else {},
            compiler_params=pltpu.CompilerParams(vmem_limit_bytes=VMEM_LIMIT),
            cost_estimate=BRIEF,
        )(*inputs)

    early = product(rights[:-1] + kept[:1] + lefts[1:-1] + kept[1:], None)
    (came_right, came_left), early = tie(((came_right, came_left), early))
    return product(rights + [came_right] + lefts[1:] + [came_left], early)


def solution(mesh):
    in_specs = (
        P(("groups", "rep", "tp"), None),
        P(None, "tp"),
        P(("groups", "rep"), "tp"),
        P(("groups", "rep"), "tp"),
        P("groups"),
        P("groups", None),
    )
    out_specs = P(("groups", "rep"), "tp")
    return jax.shard_map(local, mesh=mesh, in_specs=in_specs, out_specs=out_specs, check_vma=False)
```
